32 devices in a mesh: seq: 8 (over z, y), tp: 4 (over x, core).
Axes of the slice: x: 2, y: 2, z: 4, core: 2. Of those that a mesh axis runs over, the one named last changes fastest.
Arguments:
- patches: bfloat16 [8, 256, 1408], P('seq'), may hold values from -6 to 6
- picture_grid: int32 [8, 2], P('seq'), may hold values from 4 to 8, as said below
- vision_qkv: bfloat16 [1408, 3, 1408], P(None, None, 'tp')
- vision_out: bfloat16 [1408, 1408], P('tp'), may hold values from -0.15625 to 0.15625
- merge_weight: bfloat16 [4, 1408, 1408], P('tp'), may hold values from -0.078125 to 0.078125
- picture_block: int32 [8], P('seq'), may hold values from 0 to 7, as said below
- picture_offset: int32 [8], P('seq'), may hold values from 0 to 112, as said below
- tokens: bfloat16 [1024, 1408], P('seq', 'tp'), may hold values from -6 to 6
- prompt_lengths: int32 [16], replicated, may hold values from 1 to 256, 1024 in all
- text_qkv: bfloat16 [1408, 3, 1408], P(None, None, 'tp')
- text_out: bfloat16 [1408, 1408], P('tp'), may hold values from -0.15625 to 0.15625
Outputs:
- hidden_out: bfloat16 [1024, 1408], P('seq')
The draws below stay inside these ranges and needn't reach their ends.
Inputs may be any that keep to these rules, and one draw needn't show every extreme that they name: `picture_grid`: some picture has both entries equal to 8, another both equal to 4. `picture_block`: the blocks of different pictures differ. picture_offset plus the product of the picture's two picture_grid entries is at most 128. `prompt_lengths`: the lengths sum to 1024.
All inputs are finite; a program needn't handle non-finite values.
Results may differ from the reference program's by a relative error of at most 0.018.
Values may be sent and summed in bfloat16 or wider, within the bound.
A program may use at most 64 MiB of HBM per device.

```python
import math
import jax
import jax.numpy as jnp
import numpy as np
from jax import lax

D = 1408
HEADS = 16
HEAD = 88
MAXGRID = 16
BLOCK = 128
PROMPTS = 16
PATCHES = 256
MERGED = 64
PICTURES = 8
TOKENS = 1024
NBLOCKS = 8


def chosen_pictures(key):
    fullest = jax.random.randint(jax.random.fold_in(key, 12), (), 0, PICTURES)
    step = jax.random.randint(jax.random.fold_in(key, 15), (), 1, PICTURES)
    smallest = (fullest + step) % PICTURES
    return (fullest, smallest)


def grid_sides(key):
    halves = MAXGRID // 2
    lowest = MAXGRID // 4
    sides = jax.random.randint(jax.random.fold_in(key, 11), (PICTURES, 2), lowest, halves + 1)
    fullest, smallest = chosen_pictures(key)
    indices = jnp.arange(PICTURES)
    sides = jnp.where((indices == fullest)[:, None], halves, sides)
    return jnp.where((indices == smallest)[:, None], lowest, sides)


def draw_picture_grid(key, part):
    return grid_sides(key).astype(jnp.int32)


def draw_picture_block(key, part):
    order = jax.random.permutation(jax.random.fold_in(key, 13), NBLOCKS)
    return order[:PICTURES].astype(jnp.int32)


def draw_picture_offset(key, part):
    sides = grid_sides(key)
    room = BLOCK - sides[:, 0] * sides[:, 1] + 1
    offsets = jax.random.randint(jax.random.fold_in(key, 14), (PICTURES,), 0, room)
    fullest, smallest = chosen_pictures(key)
    indices = jnp.arange(PICTURES)
    offsets = jnp.where(indices == fullest, 0, offsets)
    offsets = jnp.where(indices == smallest, room - 1, offsets)
    return offsets.astype(jnp.int32)


def projection_draw(key):
    values = jax.random.normal(key, (D, 3, D), jnp.float32) * D ** (-0.5)
    return values.astype(jnp.bfloat16)


def draw_vision_qkv(key, part):
    return projection_draw(jax.random.fold_in(key, 21))


def draw_text_qkv(key, part):
    return projection_draw(jax.random.fold_in(key, 22))


def shard_levels(own_key, dims, cuts, low, high):
    def one(position, shards_of):
        steps = jax.random.uniform(jax.random.fold_in(jax.random.fold_in(own_key, 6), position), (shards_of,), jnp.float32, low / len(cuts), high / len(cuts))
        return jnp.repeat(jnp.exp(steps), dims[position] // shards_of).reshape((-1,) + (1,) * (len(dims) - position - 1))

    level = one(*cuts[0])
    for cut in cuts[1:]:
        level = level * one(*cut)
    return level


def length_profile(number_of, total, limit, slope):
    weights = [(1 << 20) // math.isqrt(standing ** slope) + 1 for standing in range(2, number_of + 1)]
    rest, given = total - limit - (number_of - 1), [1] * (number_of - 1)
    while rest > 0:
        free = [i for i in range(number_of - 1) if given[i] < limit]
        whole, budget = sum([weights[i] for i in free]), rest
        for i in free:
            addition = min(limit - given[i], max(1, budget * weights[i] // whole), rest)
            given[i] = given[i] + addition
            rest = rest - addition
    return np.array([limit] + given)


def uneven_parts(own_key, number_of, total, bound, slope):
    if number_of == 2:
        one = jax.random.randint(own_key, (), max(1, total - bound), min(bound, total - 1) + 1)
        return jnp.stack([one, total - one])
    sizes = jnp.asarray(length_profile(number_of, total, bound, slope), jnp.int32)
    twos = (number_of - 1) // 2
    donor, sink = sizes[1:1 + 2 * twos:2], sizes[2:2 + 2 * twos:2]
    room = jnp.minimum(donor - 1, bound - sink)
    moved = jax.random.randint(jax.random.fold_in(own_key, 1), (twos,), 0, 1 << 20) % (room + 1)
    sizes = sizes.at[1:1 + 2 * twos:2].set(donor - moved).at[2:2 + 2 * twos:2].set(sink + moved)
    return sizes[jax.random.permutation(jax.random.fold_in(own_key, 2), number_of)]


def bell_draw(stream_key, shape, scale, most, pieces=(), kind=jnp.bfloat16):
    result = scale * jax.random.normal(stream_key, shape, jnp.float32)
    if pieces:
        result = result * shard_levels(stream_key, shape, pieces, -0.22, 0.18)
    return jnp.clip(result, -most, most).astype(kind)


def setup_inputs(seed: int = 0) -> dict:
    keys = jax.random.split(jax.random.key(seed), 12)
    patches = bell_draw(keys[0], (PICTURES, PATCHES, D), 1.0, 6.0, ((0, 8),))
    picture_grid = draw_picture_grid(jax.random.fold_in(keys[11], 71), 0)
    vision_qkv = draw_vision_qkv(jax.random.fold_in(keys[11], 71), 0)
    vision_out = bell_draw(keys[3], (D, D), D ** -0.5, 0.15625, ((0, 4),))
    merge_weight = bell_draw(keys[4], (4, D, D), (4 * D) ** -0.5, 0.078125, ((0, 4),))
    picture_block = draw_picture_block(jax.random.fold_in(keys[11], 71), 0)
    picture_offset = draw_picture_offset(jax.random.fold_in(keys[11], 71), 0)
    tokens = bell_draw(keys[7], (TOKENS, D), 1.0, 6.0, ((0, 8), (1, 4)))
    prompt_lengths = uneven_parts(keys[8], PROMPTS, TOKENS, TOKENS // 4, 2).astype(jnp.int32)
    text_qkv = draw_text_qkv(jax.random.fold_in(keys[11], 71), 0)
    text_out = bell_draw(keys[10], (D, D), D ** -0.5, 0.15625, ((0, 4),))
    return {"patches": patches, "picture_grid": picture_grid, "vision_qkv": vision_qkv, "vision_out": vision_out, "merge_weight": merge_weight, "picture_block": picture_block, "picture_offset": picture_offset, "tokens": tokens, "prompt_lengths": prompt_lengths, "text_qkv": text_qkv, "text_out": text_out}


EPSILON = 1e-06
MASKED = -1e+30

def normalize(values):
    values = values.astype(jnp.float32)
    centre = lax.optimization_barrier(jnp.mean(values, axis=-1, keepdims=True))
    shifted = values - centre
    spread = lax.optimization_barrier(jnp.mean(shifted * shifted, axis=-1, keepdims=True))
    return (shifted * lax.rsqrt(spread + EPSILON)).astype(jnp.bfloat16)

def softmax_context(scores, allowed, value_rows):
    scores = jnp.where(allowed, scores, MASKED)
    row_max = lax.optimization_barrier(jnp.max(scores, axis=-1, keepdims=True))
    expons = jnp.where(allowed, jnp.exp(scores - row_max), 0.0)
    row_total = lax.optimization_barrier(jnp.sum(expons, axis=-1))
    weights = expons.astype(jnp.bfloat16)
    summed = jnp.einsum('hqk,khe->qhe', weights.astype(jnp.float32), value_rows.astype(jnp.float32))
    context = summed / jnp.transpose(row_total)[:, :, None]
    return context.astype(jnp.bfloat16).reshape(context.shape[0], -1)

def merge_cells(normed):
    halves = MAXGRID // 2
    shaped = normed.reshape(halves, 2, halves, 2, normed.shape[-1])
    return shaped.transpose(0, 2, 1, 3, 4).reshape(halves * halves, 4, normed.shape[-1])

def merged_positions(half_grid, block_index, offset):
    halves = MAXGRID // 2
    cells = jnp.arange(MERGED, dtype=jnp.int32)
    row_cell = cells // halves
    col_cell = cells % halves
    usable = (row_cell < half_grid[0]) & (col_cell < half_grid[1])
    target = block_index * BLOCK + offset + row_cell * half_grid[1] + col_cell
    return jnp.where(usable, target, -1).astype(jnp.int32)

def prompt_starts(prompt_lengths, positions):
    ends = jnp.cumsum(prompt_lengths).astype(jnp.int32)
    picked = jnp.where(ends[None, :] <= positions[:, None], prompt_lengths[None, :], 0)
    return lax.optimization_barrier(jnp.sum(picked, axis=1)).astype(jnp.int32)

def picture_layer(picture, half_grid, vision_qkv, vision_out, merge_weight):
    normed = normalize(picture)
    projected = jnp.dot(normed, vision_qkv.reshape(D, 3 * D), preferred_element_type=jnp.float32)
    projected = projected.astype(jnp.bfloat16).reshape(PATCHES, 3, HEADS, HEAD)
    scores = jnp.einsum('qhe,khe->hqk', projected[:, 0].astype(jnp.float32), projected[:, 1].astype(jnp.float32)) * HEAD ** (-0.5)
    cells = jnp.arange(PATCHES, dtype=jnp.int32)
    usable = (cells // MAXGRID < 2 * half_grid[0]) & (cells % MAXGRID < 2 * half_grid[1])
    context = softmax_context(scores, usable[None, None, :], projected[:, 2])
    hidden = picture.astype(jnp.float32) + jnp.dot(context, vision_out, preferred_element_type=jnp.float32)
    merged_in = merge_cells(normalize(hidden))
    merged = jnp.dot(merged_in.reshape(MERGED, 4 * D), merge_weight.reshape(4 * D, D), preferred_element_type=jnp.float32)
    return merged.astype(jnp.bfloat16)

def reference(patches, picture_grid, vision_qkv, vision_out, merge_weight, picture_block, picture_offset, tokens, prompt_lengths, text_qkv, text_out):

    def one_picture(index):
        return picture_layer(patches[index], picture_grid[index], vision_qkv, vision_out, merge_weight)
    merged = lax.map(one_picture, jnp.arange(PICTURES, dtype=jnp.int32))
    targets = jax.vmap(merged_positions)(picture_grid, picture_block, picture_offset).reshape(-1)
    targets = jnp.where(targets >= 0, targets, TOKENS)
    prompt_in = tokens.at[targets].set(merged.reshape(-1, D), mode='drop')
    normed = normalize(prompt_in)
    projected = jnp.dot(normed, text_qkv.reshape(D, 3 * D), preferred_element_type=jnp.float32)
    projected = projected.astype(jnp.bfloat16).reshape(TOKENS, 3, HEADS, HEAD)
    starts = prompt_starts(prompt_lengths, jnp.arange(TOKENS, dtype=jnp.int32))
    key_rows = projected[:, 1].astype(jnp.float32)
    value_rows = projected[:, 2]
    key_pos = jnp.arange(TOKENS, dtype=jnp.int32)

    def block_context(index):
        first = (index * BLOCK).astype(jnp.int32)
        query_rows = lax.dynamic_slice_in_dim(projected[:, 0], first, BLOCK, 0).astype(jnp.float32)
        query_pos = first + jnp.arange(BLOCK, dtype=jnp.int32)
        query_start = lax.dynamic_slice_in_dim(starts, first, BLOCK, 0)
        allowed = (key_pos[None, :] <= query_pos[:, None]) & (key_pos[None, :] >= query_start[:, None])
        scores = jnp.einsum('qhe,khe->hqk', query_rows, key_rows) * HEAD ** (-0.5)
        return softmax_context(scores, allowed[None], value_rows)
    contexts = lax.map(block_context, jnp.arange(TOKENS // BLOCK, dtype=jnp.int32))
    context = contexts.reshape(TOKENS, D)
    output = prompt_in.astype(jnp.float32) + jnp.dot(context, text_out, preferred_element_type=jnp.float32)
    return output.astype(jnp.bfloat16)
```

```python
import functools

import jax
import jax.numpy as jnp
from jax import lax
from jax.experimental import pallas as pl
from jax.experimental.pallas import tpu as pltpu
from jax.sharding import PartitionSpec as P

HEAD = 88
MAXGRID = 16
MERGED = 64
EPSILON = 1e-06
MASKED = -1e30
F32 = jnp.float32
BF16 = jnp.bfloat16


def normalize(values):
    values = values.astype(F32)
    centre = jnp.mean(values, axis=-1, keepdims=True)
    shifted = values - centre
    spread = jnp.mean(shifted * shifted, axis=-1, keepdims=True)
    return (shifted * lax.rsqrt(spread + EPSILON)).astype(BF16)


def matmul(a, b):
    return jnp.dot(a, b, preferred_element_type=F32)


def matmul_rows(a, b):
    return lax.dot_general(a, b, (((1,), (1,)), ((), ())), preferred_element_type=F32)


def attention(query, keys, values, allowed):
    width = query.shape[1]
    parts = [None] * (-(-width // 128))
    for head in range(width // HEAD):
        first, last = head * HEAD, (head + 1) * HEAD
        low, high = first // 128 * 128, min(width, -(-last // 128) * 128)
        lane = lax.broadcasted_iota(jnp.int32, (1, high - low), 1) + low
        inside = (lane >= first) & (lane < last)
        own_query = jnp.where(inside, query[:, low:high].astype(F32), 0.0).astype(BF16)
        own_values = jnp.where(inside, values[:, low:high].astype(F32), 0.0).astype(BF16)
        scores = matmul_rows(own_query, keys[:, low:high])
        scores = jnp.where(allowed, scores * HEAD ** (-0.5), MASKED)
        expons = jnp.exp(scores - jnp.max(scores, axis=-1, keepdims=True))
        total = jnp.sum(expons, axis=-1, keepdims=True)
        context = matmul(expons.astype(BF16), own_values) / total
        for at in range(low, high, 128):
            piece = context[:, at - low : min(high, at + 128) - low]
            slot = at // 128
            parts[slot] = piece if parts[slot] is None else parts[slot] + piece
    return [part.astype(BF16) for part in parts]


def kernel(
    seq_count,
    hops,
    patches,
    grid,
    vqkv,
    vout,
    merge,
    block,
    offset,
    tokens,
    lengths,
    tqkv,
    tout,
    out,
    patch_v,
    vqkv_v,
    vout_v,
    merge_v,
    tqkv_v,
    tout_v,
    tok_v,
    meta_v,
    context_v,
    half_send,
    half_got,
    cross_send,
    cross_got,
    term_v,
    term_got,
    gathered,
    chosen_v,
    key_v,
    value_v,
    text_context,
    last_send,
    last_got,
    load_sem,
    tok_s,
    tok_r,
    meta_s,
    meta_r,
    half_s,
    half_r,
    cross_s,
    cross_r,
    term_s,
    term_r,
    gather_s,
    gather_r,
    chosen_s,
    chosen_r,
    key_s,
    key_r,
    value_s,
    value_r,
    last_s,
    last_r,
    out_s,
    out_r,
):
    me = lax.axis_index("seq")
    t = lax.axis_index("tp")
    tp = 4
    rows = tokens.shape[0]
    width = tokens.shape[1]
    sibling = t + 1 - 2 * lax.rem(t, 2)
    across = lax.rem(t + 2, 4)
    opposite = 3 - t

    def load(source, target, index):
        copy = pltpu.make_async_copy(source, target, load_sem.at[index])
        copy.start()
        return copy

    def to_tp(source, target, send, recv, peer):
        return pltpu.make_async_remote_copy(
            src_ref=source,
            dst_ref=target,
            send_sem=send,
            recv_sem=recv,
            device_id=(me, peer),
            device_id_type=pl.DeviceIdType.MESH,
        )

    def to_seq(source, target, send, recv, peer):
        return pltpu.make_async_remote_copy(
            src_ref=source,
            dst_ref=target,
            send_sem=send,
            recv_sem=recv,
            device_id=(peer, t),
            device_id_type=pl.DeviceIdType.MESH,
        )

    load_patches = load(patches.at[0], patch_v, 0)
    load_vqkv = load(vqkv, vqkv_v, 1)
    load_vout = load(vout, vout_v, 2)
    load_merge = load(merge.at[0], merge_v, 3)
    load_tqkv = load(tqkv, tqkv_v, 4)
    load_tout = load(tout, tout_v, 5)

    barrier = pltpu.get_barrier_semaphore()
    for d in range(1, tp):
        pl.semaphore_signal(
            barrier, inc=1, device_id=(me, lax.rem(t + d, tp)), device_id_type=pl.DeviceIdType.MESH
        )

    def greet(d, _):
        pl.semaphore_signal(
            barrier,
            inc=1,
            device_id=(lax.rem(me + d, seq_count), t),
            device_id_type=pl.DeviceIdType.MESH,
        )
        return 0

    lax.fori_loop(1, seq_count, greet, 0)

    half_rows, half_cols = grid[0, 0], grid[0, 1]
    count = patch_v.shape[0]
    slot = lax.broadcasted_iota(jnp.int32, (count, count), 0)
    cell = slot % MERGED
    part = slot // MERGED
    source = (2 * (cell // 8) + part // 2) * MAXGRID + 2 * (cell % 8) + part % 2
    order = (source == lax.broadcasted_iota(jnp.int32, (count, count), 1)).astype(F32).astype(BF16)
    load_patches.wait()
    picture = matmul(order, patch_v[...]).astype(BF16)
    patch_v[...] = picture
    normed = normalize(picture)
    key_slot = lax.broadcasted_iota(jnp.int32, (1, count), 1)
    key_cell = key_slot % MERGED
    key_allowed = (key_cell // 8 < half_rows) & (key_cell % 8 < half_cols)
    load_vqkv.wait()
    query = matmul_rows(normed, vqkv_v[0]).astype(BF16)
    keys = matmul_rows(normed, vqkv_v[1]).astype(BF16)
    values = matmul_rows(normed, vqkv_v[2]).astype(BF16)
    for index, piece in enumerate(attention(query, keys, values, key_allowed)):
        context_v[:, index * 128 : index * 128 + piece.shape[1]] = piece

    field = lax.broadcasted_iota(jnp.int32, (8, 128), 0)
    meta_v[me] = jnp.where(
        field == 0,
        half_rows,
        jnp.where(field == 1, half_cols, jnp.where(field == 2, block[0], offset[0])),
    )
    tok_v[t] = tokens[...]
    pl.semaphore_wait(barrier, tp - 1 + seq_count - 1)

    load_vout.wait()

    def partial_rows(which):
        start = pl.multiple_of(which * MERGED, MERGED)
        return matmul(context_v[pl.ds(start, MERGED), :], vout_v[...])

    half_copies = []
    for index, which in ((1, opposite), (0, sibling)):
        half_send[index] = partial_rows(which).astype(BF16)
        copy = to_tp(
            half_send.at[index], half_got.at[index], half_s.at[index], half_r.at[index], sibling
        )
        copy.start()
        half_copies.append(copy)
    far = partial_rows(across)
    half_copies[0].wait_recv()
    cross_send[...] = (far + half_got[1].astype(F32)).astype(BF16)
    cross = to_tp(cross_send, cross_got, cross_s.at[0], cross_r.at[0], across)
    cross.start()
    near = partial_rows(t)
    half_copies[1].wait_recv()
    own_start = pl.multiple_of(t * MERGED, MERGED)
    hidden = (
        patch_v[pl.ds(own_start, MERGED), :].astype(F32) + near + half_got[0].astype(F32)
    )

    tok_copies = []
    for d in range(1, tp):
        copy = to_tp(tokens, tok_v.at[t], tok_s.at[d], tok_r.at[d], lax.rem(t + d, tp))
        copy.start()
        tok_copies.append(copy)

    def send_meta(d, _):
        to_seq(
            meta_v.at[me], meta_v.at[me], meta_s.at[d], meta_r.at[d], lax.rem(me + d, seq_count)
        ).start()
        return 0

    lax.fori_loop(1, seq_count, send_meta, 0)

    load_merge.wait()
    cross.wait_recv()
    merged_in = normalize(hidden + cross_got[...].astype(F32))

    share = MERGED // tp
    term_v[...] = matmul(merged_in, merge_v[...])
    term_copies = []
    for d in range(1, tp):
        peer = lax.rem(t + d, tp)
        last_send[d, 0:share, :] = term_v[
            pl.ds(pl.multiple_of(peer * share, share), share), :
        ].astype(BF16)
        copy = to_tp(
            last_send.at[d, pl.ds(0, share), :],
            term_got.at[d],
            term_s.at[d],
            term_r.at[d],
            peer,
        )
        copy.start()
        term_copies.append(copy)
    merged = term_v[pl.ds(pl.multiple_of(t * share, share), share), :]
    for d, copy in enumerate(term_copies, 1):
        copy.wait_recv()
        merged = merged + term_got[d].astype(F32)
    gathered[me] = merged.astype(BF16)

    def send_merged(d, _):
        to_seq(
            gathered.at[me],
            gathered.at[me],
            gather_s.at[d],
            gather_r.at[d],
            lax.rem(me + d, seq_count),
        ).start()
        return 0

    lax.fori_loop(1, seq_count, send_merged, 0)

    for copy in tok_copies:
        copy.wait_recv()
    token_rows = jnp.concatenate([tok_v[i].astype(F32) for i in range(tp)], axis=1)
    position = lax.broadcasted_iota(jnp.int32, (rows, 1), 0) + me * rows
    start = jnp.zeros((rows, 1), jnp.int32)
    end = jnp.int32(0)
    for index in range(lengths.shape[0]):
        end = end + lengths[index]
        start = jnp.where(end <= position, end, start)

    def meta_arrived(d, _):
        to_seq(
            meta_v.at[me], meta_v.at[me], meta_s.at[d], meta_r.at[d], lax.rem(me + d, seq_count)
        ).wait()
        return 0

    lax.fori_loop(1, seq_count, meta_arrived, 0)

    def merged_arrived(d, _):
        to_seq(
            gathered.at[me],
            gathered.at[me],
            gather_s.at[d],
            gather_r.at[d],
            lax.rem(me + d, seq_count),
        ).wait()
        return 0

    lax.fori_loop(1, seq_count, merged_arrived, 0)

    def choose(index, state):
        cells_sum, meta_sum, present = state
        about = meta_v[index]
        hit = (about[2:3, :] == me).astype(jnp.int32)
        rows_here = gathered[index].astype(F32) * hit[:, 0:1].astype(F32)
        return cells_sum + rows_here, meta_sum + about * hit, present + hit

    cells_sum, about, present = lax.fori_loop(
        0,
        seq_count,
        choose,
        (
            jnp.zeros((share, tout.shape[1]), F32),
            jnp.zeros((8, 128), jnp.int32),
            jnp.zeros((1, 128), jnp.int32),
        ),
    )
    own_cells = pl.ds(pl.multiple_of(t * share, share), share)
    chosen_v[own_cells, :] = cells_sum.astype(BF16)
    chosen_copies = []
    for d in range(1, tp):
        copy = to_tp(
            chosen_v.at[own_cells, :],
            chosen_v.at[own_cells, :],
            chosen_s.at[d],
            chosen_r.at[d],
            lax.rem(t + d, tp),
        )
        copy.start()
        chosen_copies.append(copy)

    cell = lax.broadcasted_iota(jnp.int32, (1, MERGED), 1)
    row_cell, col_cell = cell // 8, cell % 8
    g0, g1 = about[0:1, :MERGED], about[1:2, :MERGED]
    usable = (row_cell < g0) & (col_cell < g1) & (present[:, :MERGED] > 0)
    target = jnp.where(usable, about[3:4, :MERGED] + row_cell * g1 + col_cell, -1)
    table = (
        lax.broadcasted_iota(jnp.int32, (rows, MERGED), 0) == target
    ).astype(F32)
    covered = jnp.max(table, axis=1, keepdims=True)
    for copy in chosen_copies:
        copy.wait_recv()
    placed = matmul(table.astype(BF16), chosen_v[...])
    prompt_in = jnp.where(covered > 0, placed, token_rows)

    normed = normalize(prompt_in)
    load_tqkv.wait()
    key_v[0:rows, :] = matmul_rows(normed, tqkv_v[1]).astype(BF16)
    for hop in range(1, hops + 1):

        @pl.when(me + hop < seq_count)
        def _():
            to_seq(
                key_v.at[pl.ds(0, rows), :],
                key_v.at[pl.ds(hop * rows, rows), :],
                key_s.at[hop],
                key_r.at[hop],
                lax.rem(me + hop, seq_count),
            ).start()

    value_v[0:rows, :] = matmul_rows(normed, tqkv_v[2]).astype(BF16)
    for hop in range(1, hops + 1):

        @pl.when(me + hop < seq_count)
        def _():
            to_seq(
                value_v.at[pl.ds(0, rows), :],
                value_v.at[pl.ds(hop * rows, rows), :],
                value_s.at[hop],
                value_r.at[hop],
                lax.rem(me + hop, seq_count),
            ).start()

        @pl.when(me < hop)
        def _():
            key_v[hop * rows : (hop + 1) * rows, :] = jnp.zeros((rows, width), BF16)
            value_v[hop * rows : (hop + 1) * rows, :] = jnp.zeros((rows, width), BF16)

    query = matmul_rows(normed, tqkv_v[0]).astype(BF16)
    total_keys = key_v.shape[0]
    lane = lax.broadcasted_iota(jnp.int32, (1, total_keys), 1)
    key_position = (me - lane // rows) * rows + lane % rows
    visible = (key_position <= position) & (key_position >= start)
    for hop in range(1, hops + 1):

        @pl.when(me >= hop)
        def _():
            for buffer, send, recv in ((key_v, key_s, key_r), (value_v, value_s, value_r)):
                to_seq(
                    buffer.at[pl.ds(0, rows), :],
                    buffer.at[pl.ds(hop * rows, rows), :],
                    send.at[hop],
                    recv.at[hop],
                    lax.rem(me + hop, seq_count),
                ).wait_recv()

    for index, piece in enumerate(attention(query, key_v[...], value_v[...], visible)):
        text_context[:, index * 128 : index * 128 + piece.shape[1]] = piece

    for copy in term_copies:
        copy.wait_send()
    load_tout.wait()
    quarter = rows // tp
    last_copies = []
    for d in (2, 3, 1):
        peer = lax.rem(t + d, tp)
        last_send[d] = matmul(
            text_context[pl.ds(pl.multiple_of(peer * quarter, quarter), quarter), :], tout_v[...]
        ).astype(BF16)
        copy = to_tp(last_send.at[d], last_got.at[d], last_s.at[d], last_r.at[d], peer)
        copy.start()
        last_copies.append(copy)
    own_rows = pl.ds(pl.multiple_of(t * quarter, quarter), quarter)
    summed = matmul(text_context[own_rows, :], tout_v[...])
    term_v[0:quarter, :] = jnp.zeros((quarter, tout.shape[1]), F32)
    for index in range(tp):

        @pl.when(t == index)
        def _():
            term_v[0:quarter, :] = prompt_in[index * quarter : (index + 1) * quarter, :]

    summed = summed + term_v[0:quarter, :]
    for copy, d in zip(last_copies, (2, 3, 1)):
        copy.wait_recv()
        summed = summed + last_got[d].astype(F32)
    out[own_rows, :] = summed.astype(BF16)
    out_copies = []
    for d in range(1, tp):
        copy = to_tp(
            out.at[own_rows, :], out.at[own_rows, :], out_s.at[d], out_r.at[d], lax.rem(t + d, tp)
        )
        copy.start()
        out_copies.append(copy)
    for copy in tok_copies + half_copies + [cross] + chosen_copies + last_copies:
        copy.wait_send()
    for hop in range(1, hops + 1):

        @pl.when(me + hop < seq_count)
        def _():
            for buffer, send, recv in ((key_v, key_s, key_r), (value_v, value_s, value_r)):
                to_seq(
                    buffer.at[pl.ds(0, rows), :],
                    buffer.at[pl.ds(hop * rows, rows), :],
                    send.at[hop],
                    recv.at[hop],
                    lax.rem(me + hop, seq_count),
                ).wait_send()

    for copy in out_copies:
        copy.wait()


def local(
    seq_count,
    patches,
    picture_grid,
    vision_qkv,
    vision_out,
    merge_weight,
    picture_block,
    picture_offset,
    tokens,
    prompt_lengths,
    text_qkv,
    text_out,
):
    hops = (seq_count + 3) // 4
    count, model = patches.shape[1:]
    rows, width = tokens.shape
    share, quarter = MERGED // 4, rows // 4
    dma = pltpu.SemaphoreType.DMA
    anywhere = pl.BlockSpec(memory_space=pl.ANY)
    scalars = pl.BlockSpec(memory_space=pltpu.SMEM)
    vmem = pl.BlockSpec(memory_space=pltpu.VMEM)
    keys = (hops + 1) * rows
    return pl.pallas_call(
        functools.partial(kernel, seq_count, hops),
        out_shape=jax.ShapeDtypeStruct((rows, model), BF16),
        in_specs=[
            anywhere,
            scalars,
            anywhere,
            anywhere,
            anywhere,
            scalars,
            scalars,
            vmem,
            scalars,
            anywhere,
            anywhere,
        ],
        out_specs=vmem,
        scratch_shapes=[
            pltpu.VMEM((count, model), BF16),
            pltpu.VMEM((3, width, model), BF16),
            pltpu.VMEM((width, model), BF16),
            pltpu.VMEM((model, model), BF16),
            pltpu.VMEM((3, width, model), BF16),
            pltpu.VMEM((width, model), BF16),
            pltpu.VMEM((4, rows, width), BF16),
            pltpu.VMEM((seq_count, 8, 128), jnp.int32),
            pltpu.VMEM((count, width), BF16),
            pltpu.VMEM((2, MERGED, model), BF16),
            pltpu.VMEM((2, MERGED, model), BF16),
            pltpu.VMEM((MERGED, model), BF16),
            pltpu.VMEM((MERGED, model), BF16),
            pltpu.VMEM((MERGED, model), F32),
            pltpu.VMEM((4, share, model), BF16),
            pltpu.VMEM((seq_count, share, model), BF16),
            pltpu.VMEM((MERGED, model), BF16),
            pltpu.VMEM((keys, width), BF16),
            pltpu.VMEM((keys, width), BF16),
            pltpu.VMEM((rows, width), BF16),
            pltpu.VMEM((4, quarter, model), BF16),
            pltpu.VMEM((4, quarter, model), BF16),
            dma((6,)),
            dma((4,)),
            dma((4,)),
            dma((seq_count,)),
            dma((seq_count,)),
            dma((2,)),
            dma((2,)),
            dma((1,)),
            dma((1,)),
            dma((4,)),
            dma((4,)),
            dma((seq_count,)),
            dma((seq_count,)),
            dma((4,)),
            dma((4,)),
            dma((hops + 1,)),
            dma((hops + 1,)),
            dma((hops + 1,)),
            dma((hops + 1,)),
            dma((4,)),
            dma((4,)),
            dma((4,)),
            dma((4,)),
        ],
        compiler_params=pltpu.CompilerParams(
            collective_id=0, has_side_effects=True, vmem_limit_bytes=56 * 1024 * 1024
        ),
    )(
        patches,
        picture_grid,
        jnp.transpose(vision_qkv, (1, 2, 0)),
        vision_out,
        merge_weight,
        picture_block,
        picture_offset,
        tokens,
        prompt_lengths,
        jnp.transpose(text_qkv, (1, 2, 0)),
        text_out,
    )


def solution(mesh):
    placed = (
        P("seq", None, None),
        P("seq", None),
        P(None, None, "tp"),
        P("tp", None),
        P("tp", None, None),
        P("seq"),
        P("seq"),
        P("seq", "tp"),
        P(),
        P(None, None, "tp"),
        P("tp", None),
    )
    return jax.shard_map(
        functools.partial(local, mesh.shape["seq"]),
        mesh=mesh,
        in_specs=placed,
        out_specs=P("seq", None),
        check_vma=False,
    )
```

```python
import functools

import jax
import jax.numpy as jnp
from jax import lax
from jax.experimental import pallas as pl
from jax.experimental.pallas import tpu as pltpu
from jax.sharding import PartitionSpec as P

HEAD = 88
MAXGRID = 16
MERGED = 64
EPSILON = 1e-06
MASKED = -1e30
F32 = jnp.float32
BF16 = jnp.bfloat16


def normalize(values):
    values = values.astype(F32)
    centre = jnp.mean(values, axis=-1, keepdims=True)
    shifted = values - centre
    spread = jnp.mean(shifted * shifted, axis=-1, keepdims=True)
    return (shifted * lax.rsqrt(spread + EPSILON)).astype(BF16)


def matmul(a, b):
    return jnp.dot(a, b, preferred_element_type=F32)


def matmul_rows(a, b):
    return lax.dot_general(a, b, (((1,), (1,)), ((), ())), preferred_element_type=F32)


def attention(query, keys, values, allowed):
    width = query.shape[1]
    parts = [None] * (-(-width // 128))
    for head in range(width // HEAD):
        first, last = head * HEAD, (head + 1) * HEAD
        low, high = first // 128 * 128, min(width, -(-last // 128) * 128)
        lane = lax.broadcasted_iota(jnp.int32, (1, high - low), 1) + low
        inside = (lane >= first) & (lane < last)
        own_query = jnp.where(inside, query[:, low:high].astype(F32), 0.0).astype(BF16)
        own_values = jnp.where(inside, values[:, low:high].astype(F32), 0.0).astype(BF16)
        scores = matmul_rows(own_query, keys[:, low:high])
        scores = jnp.where(allowed, scores * HEAD ** (-0.5), MASKED)
        expons = jnp.exp(scores - jnp.max(scores, axis=-1, keepdims=True))
        total = jnp.sum(expons, axis=-1, keepdims=True)
        context = matmul(expons.astype(BF16), own_values) / total
        for at in range(low, high, 128):
            piece = context[:, at - low : min(high, at + 128) - low]
            slot = at // 128
            parts[slot] = piece if parts[slot] is None else parts[slot] + piece
    return [part.astype(BF16) for part in parts]


def each(count, body):
    if count <= 4:
        for index in range(count):
            body(index)
    else:

        def step(index, _):
            body(index)
            return 0

        lax.fori_loop(0, count, step, 0)


def kernel(
    seq_count,
    hops,
    patches,
    grid,
    vqkv,
    vout,
    merge,
    block,
    offset,
    tokens,
    lengths,
    tqkv,
    tout,
    out,
    patch_v,
    vqkv_v,
    vout_v,
    merge_v,
    tqkv_v,
    tout_v,
    tok_v,
    meta_v,
    context_v,
    context_got,
    cross_send,
    cross_got,
    term_v,
    term_send,
    term_got,
    gathered,
    chosen_v,
    normed_v,
    prompt_v,
    query_v,
    key_v,
    value_v,
    text_context,
    text_got,
    last_send,
    last_got,
    load_sem,
    weight_s,
    weight_r,
    tok_across_s,
    tok_across_r,
    tok_seq_s,
    tok_seq_r,
    tok_side_s,
    tok_side_r,
    meta_s,
    meta_r,
    half_s,
    half_r,
    cross_s,
    cross_r,
    term_s,
    term_r,
    gather_s,
    gather_r,
    relay_s,
    relay_r,
    chosen_s,
    chosen_r,
    last_s,
    last_r,
):
    me = lax.axis_index("seq")
    t = lax.axis_index("tp")
    tp = 4
    rows = tokens.shape[1]
    blocks = hops + 1
    sibling = t + 1 - 2 * lax.rem(t, 2)
    across = lax.rem(t + 2, 4)
    opposite = 3 - t
    partner = me + 1 - 2 * lax.rem(me, 2)

    def load(source, target, index):
        copy = pltpu.make_async_copy(source, target, load_sem.at[index])
        copy.start()
        return copy

    def remote(source, target, send, recv, device):
        return pltpu.make_async_remote_copy(
            src_ref=source,
            dst_ref=target,
            send_sem=send,
            recv_sem=recv,
            device_id=device,
            device_id_type=pl.DeviceIdType.MESH,
        )

    def to_tp(source, target, send, recv, peer):
        return remote(source, target, send, recv, (me, peer))

    def to_seq(source, target, send, recv, peer):
        return remote(source, target, send, recv, (peer, t))

    load_patches = load(patches.at[0], patch_v, 0)
    load_vqkv = load(vqkv, vqkv_v, 1)

    barrier = pltpu.get_barrier_semaphore()
    for d in range(1, tp):
        pl.semaphore_signal(
            barrier, inc=1, device_id=(me, lax.rem(t + d, tp)), device_id_type=pl.DeviceIdType.MESH
        )

    def greet(d, _):
        pl.semaphore_signal(
            barrier,
            inc=1,
            device_id=(lax.rem(me + d, seq_count), t),
            device_id_type=pl.DeviceIdType.MESH,
        )
        return 0

    lax.fori_loop(1, seq_count, greet, 0)

    half_rows, half_cols = grid[0, 0], grid[0, 1]
    count = patch_v.shape[0]
    slot = lax.broadcasted_iota(jnp.int32, (count, count), 0)
    cell = slot % MERGED
    part = slot // MERGED
    source = (2 * (cell // 8) + part // 2) * MAXGRID + 2 * (cell % 8) + part % 2
    order = (source == lax.broadcasted_iota(jnp.int32, (count, count), 1)).astype(F32).astype(BF16)
    load_patches.wait()
    picture = matmul(order, patch_v[...]).astype(BF16)
    patch_v[...] = picture
    normed = normalize(picture)
    key_slot = lax.broadcasted_iota(jnp.int32, (1, count), 1)
    key_cell = key_slot % MERGED
    key_allowed = (key_cell // 8 < half_rows) & (key_cell % 8 < half_cols)
    load_vqkv.wait()
    load_tokens = load(tokens, tok_v.at[0, t], 6)
    load_vout = load(vout, vout_v.at[0], 2)
    load_merge = load(merge.at[0], merge_v, 3)
    load_tqkv = load(tqkv, tqkv_v, 4)
    load_tout = load(tout, tout_v.at[0], 5)
    query = matmul_rows(normed, vqkv_v[0]).astype(BF16)
    keys = matmul_rows(normed, vqkv_v[1]).astype(BF16)
    values = matmul_rows(normed, vqkv_v[2]).astype(BF16)

    field = lax.broadcasted_iota(jnp.int32, (8, 128), 0)
    meta_v[me] = jnp.where(
        field == 0,
        half_rows,
        jnp.where(field == 1, half_cols, jnp.where(field == 2, block[0], offset[0])),
    )
    pl.semaphore_wait(barrier, tp - 1 + seq_count - 1)
    vout_copy = to_tp(vout, vout_v.at[1], weight_s.at[0], weight_r.at[0], sibling)
    vout_copy.start()
    tok_across = to_tp(tokens, tok_v.at[0, t], tok_across_s.at[0], tok_across_r.at[0], across)
    tok_across.start()

    def meta_copy(d):
        return to_seq(
            meta_v.at[me], meta_v.at[me], meta_s.at[d], meta_r.at[d], lax.rem(me + d, seq_count)
        )

    def send_meta(d, _):
        meta_copy(d).start()
        return 0

    lax.fori_loop(1, seq_count, send_meta, 0)

    for index, piece in enumerate(attention(query, keys, values, key_allowed)):
        context_v[:, index * 128 : index * 128 + piece.shape[1]] = piece

    def patch_rows(which):
        return pl.ds(pl.multiple_of(which * MERGED, MERGED), MERGED)

    half_copies = []
    for index, which in ((1, opposite), (0, sibling)):
        copy = to_tp(
            context_v.at[patch_rows(which), :],
            context_got.at[index],
            half_s.at[index],
            half_r.at[index],
            sibling,
        )
        copy.start()
        half_copies.append(copy)
    load_vout.wait()
    far = matmul(context_v[patch_rows(across), :], vout_v[0])
    vout_copy.wait_recv()
    half_copies[0].wait_recv()
    cross_send[...] = (far + matmul(context_got[1], vout_v[1])).astype(BF16)
    cross = to_tp(cross_send, cross_got, cross_s.at[0], cross_r.at[0], across)
    cross.start()
    near = matmul(context_v[patch_rows(t), :], vout_v[0])
    half_copies[1].wait_recv()
    near = near + matmul(context_got[0], vout_v[1])
    hidden = patch_v[patch_rows(t), :].astype(F32) + near

    tout_copy = to_tp(tout, tout_v.at[1], weight_s.at[1], weight_r.at[1], sibling)
    tout_copy.start()
    load_tokens.wait()
    tok_across.wait_recv()

    def tok_seq_copy(hop, index):
        piece = t if index == 0 else across
        return to_seq(
            tok_v.at[0, piece],
            tok_v.at[hop, piece],
            tok_seq_s.at[hop, index],
            tok_seq_r.at[hop, index],
            lax.rem(me + hop, seq_count),
        )

    def tok_side_copy(hop, index):
        piece = t if index == 0 else across
        return to_tp(
            tok_v.at[hop, piece],
            tok_v.at[hop, piece],
            tok_side_s.at[hop, index],
            tok_side_r.at[hop, index],
            sibling,
        )

    def send_tokens(hop):
        for index in range(2):
            tok_seq_copy(hop + 1, index).start()

    each(hops, send_tokens)
    for index in range(2):
        tok_side_copy(0, index).start()

    load_merge.wait()
    cross.wait_recv()
    merged_in = normalize(hidden + cross_got[...].astype(F32))

    share = MERGED // tp
    term_v[...] = matmul(merged_in, merge_v[...])
    term_copies = []
    for d in (2, 3, 1):
        peer = lax.rem(t + d, tp)
        term_send[d] = term_v[pl.ds(pl.multiple_of(peer * share, share), share), :].astype(BF16)
        copy = to_tp(term_send.at[d], term_got.at[d], term_s.at[d], term_r.at[d], peer)
        copy.start()
        term_copies.append(copy)

    def side_tokens(hop):
        for index in range(2):
            tok_seq_copy(hop + 1, index).wait()
            tok_side_copy(hop + 1, index).start()

    each(hops, side_tokens)
    merged = term_v[pl.ds(pl.multiple_of(t * share, share), share), :]
    for copy, d in zip(term_copies, (2, 3, 1)):
        copy.wait_recv()
        merged = merged + term_got[d].astype(F32)
    gathered[me] = merged.astype(BF16)

    def gather_copy(d):
        return to_seq(
            gathered.at[me],
            gathered.at[me],
            gather_s.at[d],
            gather_r.at[d],
            lax.rem(me + 2 * d, seq_count),
        )

    def relay_copy(d):
        piece = lax.rem(me + seq_count - 2 * d, seq_count)
        return to_seq(
            gathered.at[piece], gathered.at[piece], relay_s.at[d], relay_r.at[d], partner
        )

    def send_merged(d):
        gather_copy(d + 1).start()

    each(seq_count // 2 - 1, send_merged)
    relay_copy(0).start()

    def tokens_in(hop):
        for index in range(2):
            tok_side_copy(hop, index).wait()

    each(blocks, tokens_in)
    same = (
        lax.broadcasted_iota(jnp.int32, (rows, rows), 0)
        == lax.broadcasted_iota(jnp.int32, (rows, rows), 1)
    )
    same = same.astype(F32).astype(BF16)

    def block_rows(hop):
        return pl.ds(pl.multiple_of(hop * rows, rows), rows)

    def norm_tokens(hop):
        whole_rows = matmul_rows(same, tok_v[hop].reshape(-1, rows))
        normed_v[block_rows(hop), :] = normalize(whole_rows)

    each(blocks, norm_tokens)
    prompt_v[...] = matmul_rows(same, tok_v[0].reshape(-1, rows)).astype(BF16)

    def relay(d):
        gather_copy(d + 1).wait_recv()
        relay_copy(d + 1).start()

    load_tqkv.wait()
    group = 3 if blocks % 3 == 0 else 1

    def project_keys(index):
        some = pl.ds(pl.multiple_of(index * group * rows, rows), group * rows)
        key_v[some, :] = matmul_rows(normed_v[some, :], tqkv_v[1]).astype(BF16)

    def project_values(index):
        some = pl.ds(pl.multiple_of(index * group * rows, rows), group * rows)
        value_v[some, :] = matmul_rows(normed_v[some, :], tqkv_v[2]).astype(BF16)

    each(blocks // group, project_keys)
    each(seq_count // 2 - 1, relay)
    each(blocks // group, project_values)
    query_v[...] = matmul_rows(normed_v[0:rows, :], tqkv_v[0]).astype(BF16)
    position = lax.broadcasted_iota(jnp.int32, (rows, 1), 0) + me * rows
    start = jnp.zeros((rows, 1), jnp.int32)
    end = jnp.int32(0)
    for index in range(lengths.shape[0]):
        end = end + lengths[index]
        start = jnp.where(end <= position, end, start)

    def meta_arrived(d, _):
        meta_copy(d).wait()
        return 0

    lax.fori_loop(1, seq_count, meta_arrived, 0)

    def relayed(d):
        relay_copy(d).wait_recv()

    each(seq_count // 2, relayed)

    def choose(hop):
        def add(index, cells_sum):
            hit = (meta_v[index][2:3, 0:1] == me - hop).astype(F32)
            return cells_sum + gathered[index].astype(F32) * hit

        cells_sum = jnp.zeros((share, patch_v.shape[1]), F32)
        if seq_count <= 8:
            for index in range(seq_count):
                cells_sum = add(index, cells_sum)
        else:
            cells_sum = lax.fori_loop(0, seq_count, add, cells_sum)
        chosen_v[t, pl.ds(pl.multiple_of(hop * share, share), share), :] = cells_sum.astype(BF16)

    each(blocks, choose)

    def chosen_copy(index, piece, peer):
        return to_tp(
            chosen_v.at[piece], chosen_v.at[piece], chosen_s.at[index], chosen_r.at[index], peer
        )

    chosen_copies = [chosen_copy(0, t, across), chosen_copy(1, t, sibling)]
    for copy in chosen_copies:
        copy.start()

    all_cells = blocks * MERGED
    lane = lax.broadcasted_iota(jnp.int32, (1, all_cells), 1)
    lane_hop = lane % (blocks * share) // share
    lane_cell = lane // (blocks * share) * share + lane % share
    row_cell, col_cell = lane_cell // 8, lane_cell % 8

    def placement(hop):
        def add(index, state):
            about, present = state
            hit = (meta_v[index][2:3, :] == me - hop).astype(jnp.int32)
            return about + meta_v[index] * hit, present + hit

        about, present = lax.fori_loop(
            0, seq_count, add, (jnp.zeros((8, 128), jnp.int32), jnp.zeros((1, 128), jnp.int32))
        )
        g0, g1 = about[0:1, 0:1], about[1:2, 0:1]
        usable = (row_cell < g0) & (col_cell < g1) & (present[:, 0:1] > 0) & (lane_hop == hop)
        target = jnp.where(usable, about[3:4, 0:1] + row_cell * g1 + col_cell, -1)
        table = (lax.broadcasted_iota(jnp.int32, (rows, all_cells), 0) == target).astype(F32)
        return table.astype(BF16), jnp.max(table, axis=1, keepdims=True)

    if blocks <= 4:
        placements = [placement(hop) for hop in range(blocks)]

    def placement_of(hop):
        return placements[hop] if blocks <= 4 else placement(hop)

    chosen_copies[0].wait_recv()
    chosen_copies.append(chosen_copy(2, across, sibling))
    chosen_copies[2].start()
    chosen_copies[1].wait_recv()
    chosen_copies[2].wait_recv()
    cells = chosen_v[...].reshape(all_cells, -1)
    normed = normalize(cells)
    query_cells = matmul_rows(normed, tqkv_v[0]).astype(BF16)
    key_cells = matmul_rows(normed, tqkv_v[1]).astype(BF16)
    value_cells = matmul_rows(normed, tqkv_v[2]).astype(BF16)

    def put(table, covered, cells_here, before):
        return jnp.where(
            covered > 0, matmul(table, cells_here), before.astype(F32)
        ).astype(BF16)

    def put_block(hop):
        table, covered = placement_of(hop)
        here = block_rows(hop)
        key_v[here, :] = put(table, covered, key_cells, key_v[here, :])
        value_v[here, :] = put(table, covered, value_cells, value_v[here, :])

    each(blocks, put_block)
    table, covered = placement_of(0)
    query = put(table, covered, query_cells, query_v[...])

    lane = lax.broadcasted_iota(jnp.int32, (1, blocks * rows), 1)
    key_position = (me - lane // rows) * rows + lane % rows
    visible = (key_position <= position) & (key_position >= start)
    for index, piece in enumerate(attention(query, key_v[...], value_v[...], visible)):
        text_context[:, index * 128 : index * 128 + piece.shape[1]] = piece

    half = rows // 2
    core = lax.rem(t, 2)
    own_half = pl.ds(pl.multiple_of(core * half, half), half)
    side_half = pl.ds(pl.multiple_of((1 - core) * half, half), half)
    side = to_tp(text_context.at[side_half, :], text_got, last_s.at[0], last_r.at[0], sibling)
    side.start()
    load_tout.wait()
    summed = matmul(text_context[own_half, :], tout_v[0])
    tout_copy.wait_recv()
    side.wait_recv()
    summed = (summed + matmul(text_got[...], tout_v[1])).astype(BF16)
    last_send[...] = summed
    last = to_tp(last_send, last_got, last_s.at[1], last_r.at[1], across)
    last.start()
    prompt_v[...] = put(table, covered, cells, prompt_v[...])
    residual = prompt_v[own_half, :].astype(F32)
    last.wait_recv()
    total = summed.astype(F32) + last_got[...].astype(F32)
    out[own_half, :] = (residual + total).astype(BF16)
    done = to_tp(
        out.at[own_half, :], out.at[own_half, :], last_s.at[2], last_r.at[2], sibling
    )
    done.start()

    def sent(d):
        gather_copy(d + 1).wait_send()

    each(seq_count // 2 - 1, sent)

    def handed_on(d):
        relay_copy(d).wait_send()

    each(seq_count // 2, handed_on)
    for copy in [vout_copy, tout_copy, tok_across, cross, side, last]:
        copy.wait_send()
    for copy in half_copies + term_copies + chosen_copies:
        copy.wait_send()
    done.wait()


def local(
    seq_count,
    patches,
    picture_grid,
    vision_qkv,
    vision_out,
    merge_weight,
    picture_block,
    picture_offset,
    tokens,
    prompt_lengths,
    text_qkv,
    text_out,
):
    hops = (seq_count + 3) // 4
    blocks = hops + 1
    count, model = patches.shape[1:]
    rows, width = tokens.shape
    share, half = MERGED // 4, rows // 2
    dma = pltpu.SemaphoreType.DMA
    hbm = pl.BlockSpec(memory_space=pltpu.HBM)
    scalars = pl.BlockSpec(memory_space=pltpu.SMEM)
    vmem = pl.BlockSpec(memory_space=pltpu.VMEM)
    return pl.pallas_call(
        functools.partial(kernel, seq_count, hops),
        out_shape=jax.ShapeDtypeStruct((rows, model), BF16),
        in_specs=[hbm, scalars, hbm, hbm, hbm, scalars, scalars, hbm, scalars, hbm, hbm],
        out_specs=vmem,
        scratch_shapes=[
            pltpu.VMEM((count, model), BF16),
            pltpu.VMEM((3, width, model), BF16),
            pltpu.VMEM((2, width, model), BF16),
            pltpu.VMEM((model, model), BF16),
            pltpu.VMEM((3, width, model), BF16),
            pltpu.VMEM((2, width, model), BF16),
            pltpu.VMEM((blocks, 4, width, rows), BF16),
            pltpu.VMEM((seq_count, 8, 128), jnp.int32),
            pltpu.VMEM((count, width), BF16),
            pltpu.VMEM((2, MERGED, width), BF16),
            pltpu.VMEM((MERGED, model), BF16),
            pltpu.VMEM((MERGED, model), BF16),
            pltpu.VMEM((MERGED, model), F32),
            pltpu.VMEM((4, share, model), BF16),
            pltpu.VMEM((4, share, model), BF16),
            pltpu.VMEM((seq_count, share, model), BF16),
            pltpu.VMEM((4, blocks * share, model), BF16),
            pltpu.VMEM((blocks * rows, model), BF16),
            pltpu.VMEM((rows, model), BF16),
            pltpu.VMEM((rows, width), BF16),
            pltpu.VMEM((blocks * rows, width), BF16),
            pltpu.VMEM((blocks * rows, width), BF16),
            pltpu.VMEM((rows, width), BF16),
            pltpu.VMEM((half, width), BF16),
            pltpu.VMEM((half, model), BF16),
            pltpu.VMEM((half, model), BF16),
            dma((7,)),
            dma((2,)),
            dma((2,)),
            dma((1,)),
            dma((1,)),
            dma((blocks, 2)),
            dma((blocks, 2)),
            dma((blocks, 2)),
            dma((blocks, 2)),
            dma((seq_count,)),
            dma((seq_count,)),
            dma((2,)),
            dma((2,)),
            dma((1,)),
            dma((1,)),
            dma((4,)),
            dma((4,)),
            dma((seq_count,)),
            dma((seq_count,)),
            dma((seq_count,)),
            dma((seq_count,)),
            dma((3,)),
            dma((3,)),
            dma((3,)),
            dma((3,)),
        ],
        compiler_params=pltpu.CompilerParams(
            collective_id=0, has_side_effects=True, vmem_limit_bytes=56 * 1024 * 1024
        ),
    )(
        patches,
        picture_grid,
        jnp.transpose(vision_qkv, (1, 2, 0)),
        vision_out,
        merge_weight,
        picture_block,
        picture_offset,
        tokens.T,
        prompt_lengths,
        jnp.transpose(text_qkv, (1, 2, 0)),
        text_out,
    )


def solution(mesh):
    placed = (
        P("seq", None, None),
        P("seq", None),
        P(None, None, "tp"),
        P("tp", None),
        P("tp", None, None),
        P("seq"),
        P("seq"),
        P("seq", "tp"),
        P(),
        P(None, None, "tp"),
        P("tp", None),
    )
    return jax.shard_map(
        functools.partial(local, mesh.shape["seq"]),
        mesh=mesh,
        in_specs=placed,
        out_specs=P("seq", None),
        check_vma=False,
    )
```

```python
import functools

import jax
import jax.numpy as jnp
from jax import lax
from jax.experimental import pallas as pl
from jax.experimental.pallas import tpu as pltpu
from jax.sharding import PartitionSpec as P

HEAD = 88
MAXGRID = 16
MERGED = 64
EPSILON = 1e-06
MASKED = -1e30
F32 = jnp.float32
BF16 = jnp.bfloat16


def normalize(values):
    values = values.astype(F32)
    centre = jnp.mean(values, axis=-1, keepdims=True)
    shifted = values - centre
    spread = jnp.mean(shifted * shifted, axis=-1, keepdims=True)
    return (shifted * lax.rsqrt(spread + EPSILON)).astype(BF16)


def matmul(a, b):
    return jnp.dot(a, b, preferred_element_type=F32)


def matmul_rows(a, b):
    return lax.dot_general(a, b, (((1,), (1,)), ((), ())), preferred_element_type=F32)


def attention(query, keys, values, allowed):
    width = query.shape[1]
    parts = [None] * (-(-width // 128))
    for head in range(width // HEAD):
        first, last = head * HEAD, (head + 1) * HEAD
        low, high = first // 128 * 128, min(width, -(-last // 128) * 128)
        lane = lax.broadcasted_iota(jnp.int32, (1, high - low), 1) + low
        inside = (lane >= first) & (lane < last)
        own_query = jnp.where(inside, query[:, low:high].astype(F32), 0.0).astype(BF16)
        own_values = jnp.where(inside, values[:, low:high].astype(F32), 0.0).astype(BF16)
        scores = matmul_rows(own_query, keys[:, low:high])
        scores = jnp.where(allowed, scores * HEAD ** (-0.5), MASKED)
        expons = jnp.exp(scores - jnp.max(scores, axis=-1, keepdims=True))
        total = jnp.sum(expons, axis=-1, keepdims=True)
        context = matmul(expons.astype(BF16), own_values) / total
        for at in range(low, high, 128):
            piece = context[:, at - low : min(high, at + 128) - low]
            slot = at // 128
            parts[slot] = piece if parts[slot] is None else parts[slot] + piece
    return [part.astype(BF16) for part in parts]


def each(count, body):
    if count <= 4:
        for index in range(count):
            body(index)
    else:

        def step(index, _):
            body(index)
            return 0

        lax.fori_loop(0, count, step, 0)


def kernel(
    seq_count,
    hops,
    patches,
    grid,
    vqkv,
    vout,
    merge,
    block,
    offset,
    tokens,
    lengths,
    tqkv,
    tout,
    out,
    patch_v,
    vqkv_v,
    vout_v,
    merge_v,
    tqkv_v,
    tout_v,
    tok_v,
    meta_v,
    context_v,
    context_got,
    cross_send,
    cross_got,
    term_v,
    term_send,
    term_got,
    gathered,
    chosen_v,
    cells_normed,
    patch_query,
    normed_v,
    prompt_v,
    query_v,
    key_v,
    value_v,
    text_context,
    text_got,
    last_send,
    last_got,
    load_sem,
    weight_s,
    weight_r,
    tok_across_s,
    tok_across_r,
    tok_seq_s,
    tok_seq_r,
    tok_side_s,
    tok_side_r,
    meta_s,
    meta_r,
    half_s,
    half_r,
    cross_s,
    cross_r,
    term_s,
    term_r,
    gather_s,
    gather_r,
    relay_s,
    relay_r,
    chosen_s,
    chosen_r,
    last_s,
    last_r,
):
    me = lax.axis_index("seq")
    t = lax.axis_index("tp")
    tp = 4
    rows = tokens.shape[1]
    blocks = hops + 1
    sibling = t + 1 - 2 * lax.rem(t, 2)
    across = lax.rem(t + 2, 4)
    opposite = 3 - t
    partner = me + 1 - 2 * lax.rem(me, 2)

    def load(source, target, index):
        copy = pltpu.make_async_copy(source, target, load_sem.at[index])
        copy.start()
        return copy

    def remote(source, target, send, recv, device):
        return pltpu.make_async_remote_copy(
            src_ref=source,
            dst_ref=target,
            send_sem=send,
            recv_sem=recv,
            device_id=device,
            device_id_type=pl.DeviceIdType.MESH,
        )

    def to_tp(source, target, send, recv, peer):
        return remote(source, target, send, recv, (me, peer))

    def to_seq(source, target, send, recv, peer):
        return remote(source, target, send, recv, (peer, t))

    load_patches = load(patches.at[0], patch_v, 0)
    load_vqkv = load(vqkv, vqkv_v, 1)

    barrier = pltpu.get_barrier_semaphore()
    for d in range(1, tp):
        pl.semaphore_signal(
            barrier, inc=1, device_id=(me, lax.rem(t + d, tp)), device_id_type=pl.DeviceIdType.MESH
        )

    def greet(d, _):
        pl.semaphore_signal(
            barrier,
            inc=1,
            device_id=(lax.rem(me + d, seq_count), t),
            device_id_type=pl.DeviceIdType.MESH,
        )
        return 0

    lax.fori_loop(1, seq_count, greet, 0)

    half_rows, half_cols = grid[0, 0], grid[0, 1]
    count = patch_v.shape[0]
    slot = lax.broadcasted_iota(jnp.int32, (count, count), 0)
    cell = slot % MERGED
    part = slot // MERGED
    source = (2 * (cell // 8) + part // 2) * MAXGRID + 2 * (cell % 8) + part % 2
    order = (source == lax.broadcasted_iota(jnp.int32, (count, count), 1)).astype(F32).astype(BF16)
    load_patches.wait()
    picture = matmul(order, patch_v[...]).astype(BF16)
    patch_v[...] = picture
    normed = normalize(picture)
    key_slot = lax.broadcasted_iota(jnp.int32, (1, count), 1)
    key_cell = key_slot % MERGED
    key_allowed = (key_cell // 8 < half_rows) & (key_cell % 8 < half_cols)
    load_vqkv.wait()
    load_tokens = load(tokens, tok_v.at[0, t], 6)
    load_vout = load(vout, vout_v.at[0], 2)
    load_merge = load(merge.at[0], merge_v, 3)
    load_tqkv = load(tqkv, tqkv_v, 4)
    load_tout = load(tout, tout_v.at[0], 5)
    patch_query[...] = matmul_rows(normed, vqkv_v[0]).astype(BF16)
    keys = matmul_rows(normed, vqkv_v[1]).astype(BF16)
    values = matmul_rows(normed, vqkv_v[2]).astype(BF16)

    field = lax.broadcasted_iota(jnp.int32, (8, 128), 0)
    meta_v[me] = jnp.where(
        field == 0,
        half_rows,
        jnp.where(field == 1, half_cols, jnp.where(field == 2, block[0], offset[0])),
    )
    pl.semaphore_wait(barrier, tp - 1 + seq_count - 1)
    vout_copy = to_tp(vout, vout_v.at[1], weight_s.at[0], weight_r.at[0], sibling)
    vout_copy.start()
    tok_across = to_tp(tokens, tok_v.at[0, t], tok_across_s.at[0], tok_across_r.at[0], across)
    tok_across.start()

    def meta_copy(d):
        return to_seq(
            meta_v.at[me], meta_v.at[me], meta_s.at[d], meta_r.at[d], lax.rem(me + d, seq_count)
        )

    def send_meta(d, _):
        meta_copy(d).start()
        return 0

    lax.fori_loop(1, seq_count, send_meta, 0)

    def patch_rows(which):
        return pl.ds(pl.multiple_of(which * MERGED, MERGED), MERGED)

    def attend_patches(first, second):
        pair = (first, second)
        asking = jnp.concatenate([patch_query[patch_rows(which), :] for which in pair], axis=0)
        for index, piece in enumerate(attention(asking, keys, values, key_allowed)):
            lanes = pl.ds(index * 128, piece.shape[1])
            for place, which in enumerate(pair):
                context_v[patch_rows(which), lanes] = piece[place * MERGED : (place + 1) * MERGED]

    def share_context(index, which):
        copy = to_tp(
            context_v.at[patch_rows(which), :],
            context_got.at[index],
            half_s.at[index],
            half_r.at[index],
            sibling,
        )
        copy.start()
        return copy

    attend_patches(opposite, across)
    half_copies = [share_context(1, opposite)]
    load_vout.wait()
    far = matmul(context_v[patch_rows(across), :], vout_v[0])
    vout_copy.wait_recv()
    half_copies[0].wait_recv()
    cross_send[...] = (far + matmul(context_got[1], vout_v[1])).astype(BF16)
    cross = to_tp(cross_send, cross_got, cross_s.at[0], cross_r.at[0], across)
    cross.start()
    tout_copy = to_tp(tout, tout_v.at[1], weight_s.at[1], weight_r.at[1], sibling)
    tout_copy.start()
    load_tokens.wait()
    tok_across.wait_recv()

    def tok_seq_copy(hop, index):
        piece = t if index == 0 else across
        return to_seq(
            tok_v.at[0, piece],
            tok_v.at[hop, piece],
            tok_seq_s.at[hop, index],
            tok_seq_r.at[hop, index],
            lax.rem(me + hop, seq_count),
        )

    def tok_side_copy(hop, index):
        piece = t if index == 0 else across
        return to_tp(
            tok_v.at[hop, piece],
            tok_v.at[hop, piece],
            tok_side_s.at[hop, index],
            tok_side_r.at[hop, index],
            sibling,
        )

    def send_tokens(hop):
        for index in range(2):
            tok_seq_copy(hop + 1, index).start()

    each(hops, send_tokens)
    for index in range(2):
        tok_side_copy(0, index).start()

    attend_patches(sibling, t)
    half_copies.append(share_context(0, sibling))
    near = matmul(context_v[patch_rows(t), :], vout_v[0])
    half_copies[1].wait_recv()
    near = near + matmul(context_got[0], vout_v[1])
    hidden = patch_v[patch_rows(t), :].astype(F32) + near

    load_merge.wait()
    cross.wait_recv()
    merged_in = normalize(hidden + cross_got[...].astype(F32))

    share = MERGED // tp
    term_v[...] = matmul(merged_in, merge_v[...])
    term_copies = []
    for d in (2, 3, 1):
        peer = lax.rem(t + d, tp)
        term_send[d] = term_v[pl.ds(pl.multiple_of(peer * share, share), share), :].astype(BF16)
        copy = to_tp(term_send.at[d], term_got.at[d], term_s.at[d], term_r.at[d], peer)
        copy.start()
        term_copies.append(copy)

    def side_tokens(hop):
        for index in range(2):
            tok_seq_copy(hop + 1, index).wait()
            tok_side_copy(hop + 1, index).start()

    def tokens_in(hop):
        for index in range(2):
            tok_side_copy(hop, index).wait()

    same = (
        lax.broadcasted_iota(jnp.int32, (rows, rows), 0)
        == lax.broadcasted_iota(jnp.int32, (rows, rows), 1)
    )
    same = same.astype(F32).astype(BF16)

    def block_rows(hop):
        return pl.ds(pl.multiple_of(hop * rows, rows), rows)

    def norm_tokens(hop):
        whole_rows = matmul_rows(same, tok_v[hop].reshape(-1, rows))
        normed_v[block_rows(hop), :] = normalize(whole_rows)
        return whole_rows

    tokens_in(0)
    prompt_v[...] = norm_tokens(0).astype(BF16)
    merged = term_v[pl.ds(pl.multiple_of(t * share, share), share), :]
    for copy, d in zip(term_copies, (2, 3, 1)):
        copy.wait_recv()
        merged = merged + term_got[d].astype(F32)
    gathered[me] = merged.astype(BF16)

    def gather_copy(d):
        return to_seq(
            gathered.at[me],
            gathered.at[me],
            gather_s.at[d],
            gather_r.at[d],
            lax.rem(me + 2 * d, seq_count),
        )

    def relay_copy(d):
        piece = lax.rem(me + seq_count - 2 * d, seq_count)
        return to_seq(
            gathered.at[piece], gathered.at[piece], relay_s.at[d], relay_r.at[d], partner
        )

    def send_merged(d):
        gather_copy(d + 1).start()

    each(seq_count // 2 - 1, send_merged)
    relay_copy(0).start()

    each(hops, side_tokens)
    load_tqkv.wait()
    query_v[...] = matmul_rows(normed_v[0:rows, :], tqkv_v[0]).astype(BF16)

    def relay(d):
        gather_copy(d + 1).wait_recv()
        relay_copy(d + 1).start()

    def norm_earlier(hop):
        tokens_in(hop + 1)
        norm_tokens(hop + 1)

    each(seq_count // 2 - 1, relay)
    each(hops, norm_earlier)
    group = 3 if blocks % 3 == 0 else 1

    def project(index):
        some = pl.ds(pl.multiple_of(index * group * rows, rows), group * rows)
        key_v[some, :] = matmul_rows(normed_v[some, :], tqkv_v[1]).astype(BF16)
        value_v[some, :] = matmul_rows(normed_v[some, :], tqkv_v[2]).astype(BF16)

    each(blocks // group, project)
    half = rows // 2
    core = lax.rem(t, 2)

    def visible_to(which):
        position = lax.broadcasted_iota(jnp.int32, (half, 1), 0) + me * rows + which * half
        start = jnp.zeros((half, 1), jnp.int32)
        end = jnp.int32(0)
        for index in range(lengths.shape[0]):
            end = end + lengths[index]
            start = jnp.where(end <= position, end, start)
        lane = lax.broadcasted_iota(jnp.int32, (1, blocks * rows), 1)
        key_position = (me - lane // rows) * rows + lane % rows
        return (key_position <= position) & (key_position >= start)

    def meta_arrived(d, _):
        meta_copy(d).wait()
        return 0

    lax.fori_loop(1, seq_count, meta_arrived, 0)

    def relayed(d):
        relay_copy(d).wait_recv()

    each(seq_count // 2, relayed)

    def choose(hop):
        def add(index, cells_sum):
            hit = (meta_v[index][2:3, 0:1] == me - hop).astype(F32)
            return cells_sum + gathered[index].astype(F32) * hit

        cells_sum = jnp.zeros((share, patch_v.shape[1]), F32)
        if seq_count <= 8:
            for index in range(seq_count):
                cells_sum = add(index, cells_sum)
        else:
            cells_sum = lax.fori_loop(0, seq_count, add, cells_sum)
        chosen_v[t, pl.ds(pl.multiple_of(hop * share, share), share), :] = cells_sum.astype(BF16)

    each(blocks, choose)

    def chosen_copy(index, piece, peer):
        return to_tp(
            chosen_v.at[piece], chosen_v.at[piece], chosen_s.at[index], chosen_r.at[index], peer
        )

    chosen_copies = [chosen_copy(0, t, across), chosen_copy(1, t, sibling)]
    for copy in chosen_copies:
        copy.start()

    all_cells = blocks * MERGED
    lane = lax.broadcasted_iota(jnp.int32, (1, all_cells), 1)
    lane_hop = lane % (blocks * share) // share
    lane_cell = lane // (blocks * share) * share + lane % share
    row_cell, col_cell = lane_cell // 8, lane_cell % 8

    def placement(hop):
        def add(index, state):
            about, present = state
            hit = (meta_v[index][2:3, :] == me - hop).astype(jnp.int32)
            return about + meta_v[index] * hit, present + hit

        about, present = lax.fori_loop(
            0, seq_count, add, (jnp.zeros((8, 128), jnp.int32), jnp.zeros((1, 128), jnp.int32))
        )
        g0, g1 = about[0:1, 0:1], about[1:2, 0:1]
        usable = (row_cell < g0) & (col_cell < g1) & (present[:, 0:1] > 0) & (lane_hop == hop)
        target = jnp.where(usable, about[3:4, 0:1] + row_cell * g1 + col_cell, -1)
        table = (lax.broadcasted_iota(jnp.int32, (rows, all_cells), 0) == target).astype(F32)
        return table.astype(BF16), jnp.max(table, axis=1, keepdims=True)

    if blocks <= 4:
        placements = [placement(hop) for hop in range(blocks)]

    def placement_of(hop):
        return placements[hop] if blocks <= 4 else placement(hop)

    cells_normed[t] = normalize(chosen_v[t])
    chosen_copies[1].wait_recv()
    cells_normed[sibling] = normalize(chosen_v[sibling])
    chosen_copies[0].wait_recv()
    chosen_copies.append(chosen_copy(2, across, sibling))
    chosen_copies[2].start()
    cells_normed[across] = normalize(chosen_v[across])
    chosen_copies[2].wait_recv()
    cells_normed[opposite] = normalize(chosen_v[opposite])
    normed = cells_normed[...].reshape(all_cells, -1)
    query_cells = matmul_rows(normed, tqkv_v[0]).astype(BF16)
    key_cells = matmul_rows(normed, tqkv_v[1]).astype(BF16)
    value_cells = matmul_rows(normed, tqkv_v[2]).astype(BF16)

    def put(table, covered, cells_here, before):
        return jnp.where(
            covered > 0, matmul(table, cells_here), before.astype(F32)
        ).astype(BF16)

    def put_block(hop):
        table, covered = placement_of(hop)
        here = block_rows(hop)
        key_v[here, :] = put(table, covered, key_cells, key_v[here, :])
        value_v[here, :] = put(table, covered, value_cells, value_v[here, :])

    each(blocks, put_block)
    table, covered = placement_of(0)
    query_v[...] = put(table, covered, query_cells, query_v[...])

    own_half = pl.ds(pl.multiple_of(core * half, half), half)
    side_half = pl.ds(pl.multiple_of((1 - core) * half, half), half)

    def attend_half(which, here):
        visible = visible_to(which)
        pieces = attention(query_v[here, :], key_v[...], value_v[...], visible)
        for index, piece in enumerate(pieces):
            text_context[here, pl.ds(index * 128, piece.shape[1])] = piece

    attend_half(1 - core, side_half)
    side = to_tp(text_context.at[side_half, :], text_got, last_s.at[0], last_r.at[0], sibling)
    side.start()
    attend_half(core, own_half)
    load_tout.wait()
    summed = matmul(text_context[own_half, :], tout_v[0])
    tout_copy.wait_recv()
    side.wait_recv()
    summed = (summed + matmul(text_got[...], tout_v[1])).astype(BF16)
    last_send[...] = summed
    last = to_tp(last_send, last_got, last_s.at[1], last_r.at[1], across)
    last.start()
    prompt_v[...] = put(table, covered, chosen_v[...].reshape(all_cells, -1), prompt_v[...])
    residual = prompt_v[own_half, :].astype(F32)
    last.wait_recv()
    total = summed.astype(F32) + last_got[...].astype(F32)
    out[own_half, :] = (residual + total).astype(BF16)
    done = to_tp(
        out.at[own_half, :], out.at[own_half, :], last_s.at[2], last_r.at[2], sibling
    )
    done.start()

    def sent(d):
        gather_copy(d + 1).wait_send()

    each(seq_count // 2 - 1, sent)

    def handed_on(d):
        relay_copy(d).wait_send()

    each(seq_count // 2, handed_on)
    for copy in [vout_copy, tout_copy, tok_across, cross, side, last]:
        copy.wait_send()
    for copy in half_copies + term_copies + chosen_copies:
        copy.wait_send()
    done.wait()


def local(
    seq_count,
    patches,
    picture_grid,
    vision_qkv,
    vision_out,
    merge_weight,
    picture_block,
    picture_offset,
    tokens,
    prompt_lengths,
    text_qkv,
    text_out,
):
    hops = (seq_count + 3) // 4
    blocks = hops + 1
    count, model = patches.shape[1:]
    rows, width = tokens.shape
    share, half = MERGED // 4, rows // 2
    dma = pltpu.SemaphoreType.DMA
    hbm = pl.BlockSpec(memory_space=pltpu.HBM)
    scalars = pl.BlockSpec(memory_space=pltpu.SMEM)
    vmem = pl.BlockSpec(memory_space=pltpu.VMEM)
    return pl.pallas_call(
        functools.partial(kernel, seq_count, hops),
        out_shape=pltpu.VMEM((rows, model), BF16),
        in_specs=[hbm, scalars, hbm, hbm, hbm, scalars, scalars, hbm, scalars, hbm, hbm],
        out_specs=vmem,
        scratch_shapes=[
            pltpu.VMEM((count, model), BF16),
            pltpu.VMEM((3, width, model), BF16),
            pltpu.VMEM((2, width, model), BF16),
            pltpu.VMEM((model, model), BF16),
            pltpu.VMEM((3, width, model), BF16),
            pltpu.VMEM((2, width, model), BF16),
            pltpu.VMEM((blocks, 4, width, rows), BF16),
            pltpu.VMEM((seq_count, 8, 128), jnp.int32),
            pltpu.VMEM((count, width), BF16),
            pltpu.VMEM((2, MERGED, width), BF16),
            pltpu.VMEM((MERGED, model), BF16),
            pltpu.VMEM((MERGED, model), BF16),
            pltpu.VMEM((MERGED, model), F32),
            pltpu.VMEM((4, share, model), BF16),
            pltpu.VMEM((4, share, model), BF16),
            pltpu.VMEM((seq_count, share, model), BF16),
            pltpu.VMEM((4, blocks * share, model), BF16),
            pltpu.VMEM((4, blocks * share, model), BF16),
            pltpu.VMEM((count, width), BF16),
            pltpu.VMEM((blocks * rows, model), BF16),
            pltpu.VMEM((rows, model), BF16),
            pltpu.VMEM((rows, width), BF16),
            pltpu.VMEM((blocks * rows, width), BF16),
            pltpu.VMEM((blocks * rows, width), BF16),
            pltpu.VMEM((rows, width), BF16),
            pltpu.VMEM((half, width), BF16),
            pltpu.VMEM((half, model), BF16),
            pltpu.VMEM((half, model), BF16),
            dma((7,)),
            dma((2,)),
            dma((2,)),
            dma((1,)),
            dma((1,)),
            dma((blocks, 2)),
            dma((blocks, 2)),
            dma((blocks, 2)),
            dma((blocks, 2)),
            dma((seq_count,)),
            dma((seq_count,)),
            dma((2,)),
            dma((2,)),
            dma((1,)),
            dma((1,)),
            dma((4,)),
            dma((4,)),
            dma((seq_count,)),
            dma((seq_count,)),
            dma((seq_count,)),
            dma((seq_count,)),
            dma((3,)),
            dma((3,)),
            dma((3,)),
            dma((3,)),
        ],
        compiler_params=pltpu.CompilerParams(
            collective_id=0, has_side_effects=True, vmem_limit_bytes=56 * 1024 * 1024
        ),
    )(
        patches,
        picture_grid,
        jnp.transpose(vision_qkv, (1, 2, 0)),
        vision_out,
        merge_weight,
        picture_block,
        picture_offset,
        tokens.T,
        prompt_lengths,
        jnp.transpose(text_qkv, (1, 2, 0)),
        text_out,
    )


def solution(mesh):
    placed = (
        P("seq", None, None),
        P("seq", None),
        P(None, None, "tp"),
        P("tp", None),
        P("tp", None, None),
        P("seq"),
        P("seq"),
        P("seq", "tp"),
        P(),
        P(None, None, "tp"),
        P("tp", None),
    )
    return jax.shard_map(
        functools.partial(local, mesh.shape["seq"]),
        mesh=mesh,
        in_specs=placed,
        out_specs=P("seq", None),
        check_vma=False,
    )
```

```python
import functools

import jax
import jax.numpy as jnp
from jax import lax
from jax.experimental import pallas as pl
from jax.experimental.pallas import tpu as pltpu
from jax.sharding import PartitionSpec as P

HEAD = 88
MAXGRID = 16
MERGED = 64
EPSILON = 1e-06
MASKED = -1e31
LOG2E = 1.4426950408889634
F32 = jnp.float32
BF16 = jnp.bfloat16


def normalize(values):
    values = values.astype(F32)
    centre = jnp.mean(values, axis=-1, keepdims=True)
    shifted = values - centre
    spread = jnp.mean(shifted * shifted, axis=-1, keepdims=True)
    return (shifted * lax.rsqrt(spread + EPSILON)).astype(BF16)


def matmul(a, b):
    return jnp.dot(a, b, preferred_element_type=F32)


def matmul_rows(a, b):
    return lax.dot_general(a, b, (((1,), (1,)), ((), ())), preferred_element_type=F32)


def attention(query, keys, values, allowed):
    width = query.shape[1]
    parts = [None] * (-(-width // 128))
    for head in range(width // HEAD):
        first, last = head * HEAD, (head + 1) * HEAD
        low, high = first // 128 * 128, min(width, -(-last // 128) * 128)
        lane = lax.broadcasted_iota(jnp.int32, (1, high - low), 1) + low
        inside = ((lane >= first) & (lane < last)).astype(F32).astype(BF16)
        scores = matmul_rows(query[:, low:high] * inside, keys[:, low:high])
        scores = jnp.where(allowed, scores, MASKED)
        top = jnp.max(scores, axis=-1, keepdims=True)
        expons = jnp.exp2((scores - top) * (HEAD ** (-0.5) * LOG2E))
        total = jnp.sum(expons, axis=-1, keepdims=True)
        context = matmul(expons.astype(BF16), values[:, low:high] * inside) * (1.0 / total)
        for at in range(low, high, 128):
            piece = context[:, at - low : min(high, at + 128) - low]
            slot = at // 128
            parts[slot] = piece if parts[slot] is None else parts[slot] + piece
    return [part.astype(BF16) for part in parts]


def each(count, body):
    if count <= 4:
        for index in range(count):
            body(index)
    else:

        def step(index, _):
            body(index)
            return 0

        lax.fori_loop(0, count, step, 0)


def kernel(
    seq_count,
    hops,
    patches,
    grid,
    vqkv,
    vout,
    merge,
    block,
    offset,
    tokens,
    lengths,
    tqkv,
    tout,
    out,
    patch_v,
    vqkv_v,
    vout_v,
    merge_v,
    tqkv_v,
    tout_v,
    tok_v,
    meta_v,
    context_v,
    context_got,
    cross_send,
    cross_got,
    term_v,
    term_send,
    term_got,
    gathered,
    chosen_v,
    cells_normed,
    patch_query,
    normed_v,
    prompt_v,
    query_v,
    key_v,
    value_v,
    text_context,
    text_got,
    last_send,
    last_got,
    load_sem,
    weight_s,
    weight_r,
    tok_across_s,
    tok_across_r,
    tok_seq_s,
    tok_seq_r,
    tok_side_s,
    tok_side_r,
    meta_s,
    meta_r,
    half_s,
    half_r,
    cross_s,
    cross_r,
    term_s,
    term_r,
    gather_s,
    gather_r,
    relay_s,
    relay_r,
    chosen_s,
    chosen_r,
    last_s,
    last_r,
):
    me = lax.axis_index("seq")
    t = lax.axis_index("tp")
    tp = 4
    rows = tokens.shape[1]
    blocks = hops + 1
    sibling = t + 1 - 2 * lax.rem(t, 2)
    across = lax.rem(t + 2, 4)
    opposite = 3 - t
    partner = me + 1 - 2 * lax.rem(me, 2)

    def load(source, target, index):
        copy = pltpu.make_async_copy(source, target, load_sem.at[index])
        copy.start()
        return copy

    def remote(source, target, send, recv, device):
        return pltpu.make_async_remote_copy(
            src_ref=source,
            dst_ref=target,
            send_sem=send,
            recv_sem=recv,
            device_id=device,
            device_id_type=pl.DeviceIdType.MESH,
        )

    def to_tp(source, target, send, recv, peer):
        return remote(source, target, send, recv, (me, peer))

    def to_seq(source, target, send, recv, peer):
        return remote(source, target, send, recv, (peer, t))

    load_patches = load(patches.at[0], patch_v, 0)
    load_vqkv = load(vqkv, vqkv_v, 1)

    barrier = pltpu.get_barrier_semaphore()
    for d in range(1, tp):
        pl.semaphore_signal(
            barrier, inc=1, device_id=(me, lax.rem(t + d, tp)), device_id_type=pl.DeviceIdType.MESH
        )

    def greet(d, _):
        pl.semaphore_signal(
            barrier,
            inc=1,
            device_id=(lax.rem(me + d, seq_count), t),
            device_id_type=pl.DeviceIdType.MESH,
        )
        return 0

    lax.fori_loop(1, seq_count, greet, 0)

    half_rows, half_cols = grid[0, 0], grid[0, 1]
    count = patch_v.shape[0]

    def ordering(first, size):
        slot = lax.broadcasted_iota(jnp.int32, (size, count), 0) + first
        cell = slot % MERGED
        part = slot // MERGED
        source = (2 * (cell // 8) + part // 2) * MAXGRID + 2 * (cell % 8) + part % 2
        picked = source == lax.broadcasted_iota(jnp.int32, (size, count), 1)
        return picked.astype(F32).astype(BF16)

    order = ordering(0, count)
    key_slot = lax.broadcasted_iota(jnp.int32, (1, count), 1)
    key_allowed = (key_slot // MAXGRID < 2 * half_rows) & (key_slot % MAXGRID < 2 * half_cols)
    load_patches.wait()
    normed = normalize(patch_v[...])

    pl.semaphore_wait(barrier, tp - 1 + seq_count - 1)
    tok_across = to_tp(tokens, tok_v.at[0, t], tok_across_s.at[0], tok_across_r.at[0], across)
    tok_across.start()
    load_tokens = load(tokens, tok_v.at[0, t], 6)

    def tok_seq_copy(hop, index):
        piece = t if index == 0 else across
        return to_seq(
            tok_v.at[0, piece],
            tok_v.at[hop, piece],
            tok_seq_s.at[hop, index],
            tok_seq_r.at[hop, index],
            lax.rem(me + hop, seq_count),
        )

    def tok_side_copy(hop, index):
        piece = t if index == 0 else across
        return to_tp(
            tok_v.at[hop, piece],
            tok_v.at[hop, piece],
            tok_side_s.at[hop, index],
            tok_side_r.at[hop, index],
            sibling,
        )

    def send_own(hop):
        tok_seq_copy(hop + 1, 0).start()

    def send_across(hop):
        tok_seq_copy(hop + 1, 1).start()

    load_vqkv.wait()
    load_vout = load(vout, vout_v.at[0], 2)
    load_merge = load(merge.at[0], merge_v, 3)
    load_tokens.wait()
    each(hops, send_own)
    vout_copy = to_tp(vout, vout_v.at[1], weight_s.at[0], weight_r.at[0], sibling)
    vout_copy.start()
    load_tqkv = load(tqkv, tqkv_v, 4)
    load_tout = load(tout, tout_v.at[0], 5)
    query = matmul_rows(normed, vqkv_v[0]).astype(BF16)
    patch_query[...] = matmul(order, query).astype(BF16)
    keys = matmul_rows(normed, vqkv_v[1]).astype(BF16)
    values = matmul_rows(normed, vqkv_v[2]).astype(BF16)
    tok_across.wait_recv()
    each(hops, send_across)
    for index in range(2):
        tok_side_copy(0, index).start()

    def meta_copy(d):
        return to_seq(
            meta_v.at[me], meta_v.at[me], meta_s.at[d], meta_r.at[d], lax.rem(me + d, seq_count)
        )

    def patch_rows(which):
        return pl.ds(pl.multiple_of(which * MERGED, MERGED), MERGED)

    def attend_patches(first, second):
        pair = (first, second)
        asking = jnp.concatenate([patch_query[patch_rows(which), :] for which in pair], axis=0)
        for index, piece in enumerate(attention(asking, keys, values, key_allowed)):
            lanes = pl.ds(index * 128, piece.shape[1])
            for place, which in enumerate(pair):
                context_v[patch_rows(which), lanes] = piece[place * MERGED : (place + 1) * MERGED]

    def share_context(index, which):
        copy = to_tp(
            context_v.at[patch_rows(which), :],
            context_got.at[index],
            half_s.at[index],
            half_r.at[index],
            sibling,
        )
        copy.start()
        return copy

    attend_patches(opposite, across)
    half_copies = [share_context(1, opposite)]
    load_vout.wait()
    far = matmul(context_v[patch_rows(across), :], vout_v[0])
    vout_copy.wait_recv()
    half_copies[0].wait_recv()
    cross_send[...] = (far + matmul(context_got[1], vout_v[1])).astype(BF16)
    cross = to_tp(cross_send, cross_got, cross_s.at[0], cross_r.at[0], across)
    cross.start()
    attend_patches(sibling, t)
    half_copies.append(share_context(0, sibling))
    near = matmul(context_v[patch_rows(t), :], vout_v[0])
    half_copies[1].wait_recv()
    near = near + matmul(context_got[0], vout_v[1])
    hidden = matmul(ordering(t * MERGED, MERGED), patch_v[...]) + near
    tout_copy = to_tp(tout, tout_v.at[1], weight_s.at[1], weight_r.at[1], sibling)
    tout_copy.start()

    field = lax.broadcasted_iota(jnp.int32, (8, 128), 0)
    meta_v[me] = jnp.where(
        field == 0,
        half_rows,
        jnp.where(field == 1, half_cols, jnp.where(field == 2, block[0], offset[0])),
    )

    def send_meta(d, _):
        meta_copy(d).start()
        return 0

    lax.fori_loop(1, seq_count, send_meta, 0)

    same = (
        lax.broadcasted_iota(jnp.int32, (rows, rows), 0)
        == lax.broadcasted_iota(jnp.int32, (rows, rows), 1)
    )
    same = same.astype(F32).astype(BF16)

    def block_rows(hop):
        return pl.ds(pl.multiple_of(hop * rows, rows), rows)

    def norm_tokens(hop):
        whole_rows = matmul_rows(same, tok_v[hop].reshape(-1, rows))
        normed_v[block_rows(hop), :] = normalize(whole_rows)
        return whole_rows

    def tokens_in(hop):
        for index in range(2):
            tok_side_copy(hop, index).wait()

    tokens_in(0)
    prompt_v[...] = norm_tokens(0).astype(BF16)

    load_merge.wait()
    cross.wait_recv()
    merged_in = normalize(hidden + cross_got[...].astype(F32))

    share = MERGED // tp
    term_v[...] = matmul(merged_in, merge_v[...])
    term_copies = []
    for d in (2, 3, 1):
        peer = lax.rem(t + d, tp)
        term_send[d] = term_v[pl.ds(pl.multiple_of(peer * share, share), share), :].astype(BF16)
        copy = to_tp(term_send.at[d], term_got.at[d], term_s.at[d], term_r.at[d], peer)
        copy.start()
        term_copies.append(copy)

    def side_tokens(hop):
        for index in range(2):
            tok_seq_copy(hop + 1, index).wait()
            tok_side_copy(hop + 1, index).start()

    each(hops, side_tokens)
    merged = term_v[pl.ds(pl.multiple_of(t * share, share), share), :]
    for copy, d in zip(term_copies, (2, 3, 1)):
        copy.wait_recv()
        merged = merged + term_got[d].astype(F32)
    gathered[me] = merged.astype(BF16)

    def gather_copy(d):
        return to_seq(
            gathered.at[me],
            gathered.at[me],
            gather_s.at[d],
            gather_r.at[d],
            lax.rem(me + 2 * d, seq_count),
        )

    def relay_copy(d):
        piece = lax.rem(me + seq_count - 2 * d, seq_count)
        return to_seq(
            gathered.at[piece], gathered.at[piece], relay_s.at[d], relay_r.at[d], partner
        )

    def send_merged(d):
        gather_copy(d + 1).start()

    each(seq_count // 2 - 1, send_merged)
    relay_copy(0).start()

    load_tqkv.wait()
    query_v[...] = matmul_rows(normed_v[0:rows, :], tqkv_v[0]).astype(BF16)

    def relay(d):
        gather_copy(d + 1).wait_recv()
        relay_copy(d + 1).start()

    def norm_earlier(hop):
        tokens_in(hop + 1)
        norm_tokens(hop + 1)

    each(seq_count // 2 - 1, relay)
    each(hops, norm_earlier)
    group = 3 if blocks % 3 == 0 else 1

    def project(index):
        some = pl.ds(pl.multiple_of(index * group * rows, rows), group * rows)
        key_v[some, :] = matmul_rows(normed_v[some, :], tqkv_v[1]).astype(BF16)
        value_v[some, :] = matmul_rows(normed_v[some, :], tqkv_v[2]).astype(BF16)

    each(blocks // group, project)
    half = rows // 2
    core = lax.rem(t, 2)

    def visible_to(which):
        position = lax.broadcasted_iota(jnp.int32, (half, 1), 0) + me * rows + which * half
        start = jnp.zeros((half, 1), jnp.int32)
        end = jnp.int32(0)
        for index in range(lengths.shape[0]):
            end = end + lengths[index]
            start = jnp.where(end <= position, end, start)
        lane = lax.broadcasted_iota(jnp.int32, (1, blocks * rows), 1)
        key_position = (me - lane // rows) * rows + lane % rows
        return (key_position <= position) & (key_position >= start)

    def meta_arrived(d, _):
        meta_copy(d).wait()
        return 0

    lax.fori_loop(1, seq_count, meta_arrived, 0)

    def relayed(d):
        relay_copy(d).wait_recv()

    each(seq_count // 2, relayed)

    def choose(hop):
        def add(index, cells_sum):
            hit = (meta_v[index][2:3, 0:1] == me - hop).astype(F32)
            return cells_sum + gathered[index].astype(F32) * hit

        cells_sum = jnp.zeros((share, patch_v.shape[1]), F32)
        if seq_count <= 8:
            for index in range(seq_count):
                cells_sum = add(index, cells_sum)
        else:
            cells_sum = lax.fori_loop(0, seq_count, add, cells_sum)
        chosen_v[t, pl.ds(pl.multiple_of(hop * share, share), share), :] = cells_sum.astype(BF16)

    each(blocks, choose)

    def chosen_copy(index, piece, peer):
        return to_tp(
            chosen_v.at[piece], chosen_v.at[piece], chosen_s.at[index], chosen_r.at[index], peer
        )

    chosen_copies = [chosen_copy(0, t, across), chosen_copy(1, t, sibling)]
    for copy in chosen_copies:
        copy.start()

    all_cells = blocks * MERGED
    lane = lax.broadcasted_iota(jnp.int32, (1, all_cells), 1)
    lane_hop = lane % (blocks * share) // share
    lane_cell = lane // (blocks * share) * share + lane % share
    row_cell, col_cell = lane_cell // 8, lane_cell % 8

    def placement(hop):
        def add(index, state):
            about, present = state
            hit = (meta_v[index][2:3, :] == me - hop).astype(jnp.int32)
            return about + meta_v[index] * hit, present + hit

        about, present = lax.fori_loop(
            0, seq_count, add, (jnp.zeros((8, 128), jnp.int32), jnp.zeros((1, 128), jnp.int32))
        )
        g0, g1 = about[0:1, 0:1], about[1:2, 0:1]
        usable = (row_cell < g0) & (col_cell < g1) & (present[:, 0:1] > 0) & (lane_hop == hop)
        target = jnp.where(usable, about[3:4, 0:1] + row_cell * g1 + col_cell, -1)
        table = (lax.broadcasted_iota(jnp.int32, (rows, all_cells), 0) == target).astype(F32)
        return table.astype(BF16), jnp.max(table, axis=1, keepdims=True)

    if blocks <= 4:
        placements = [placement(hop) for hop in range(blocks)]

    def placement_of(hop):
        return placements[hop] if blocks <= 4 else placement(hop)

    cells_normed[t] = normalize(chosen_v[t])
    chosen_copies[1].wait_recv()
    cells_normed[sibling] = normalize(chosen_v[sibling])
    chosen_copies[0].wait_recv()
    chosen_copies.append(chosen_copy(2, across, sibling))
    chosen_copies[2].start()
    cells_normed[across] = normalize(chosen_v[across])
    chosen_copies[2].wait_recv()
    cells_normed[opposite] = normalize(chosen_v[opposite])
    normed = cells_normed[...].reshape(all_cells, -1)
    query_cells = matmul_rows(normed, tqkv_v[0]).astype(BF16)
    key_cells = matmul_rows(normed, tqkv_v[1]).astype(BF16)
    value_cells = matmul_rows(normed, tqkv_v[2]).astype(BF16)

    def put(table, covered, cells_here, before):
        return jnp.where(
            covered > 0, matmul(table, cells_here), before.astype(F32)
        ).astype(BF16)

    def put_block(hop):
        table, covered = placement_of(hop)
        here = block_rows(hop)
        key_v[here, :] = put(table, covered, key_cells, key_v[here, :])
        value_v[here, :] = put(table, covered, value_cells, value_v[here, :])

    each(blocks, put_block)
    table, covered = placement_of(0)
    query_v[...] = put(table, covered, query_cells, query_v[...])

    own_half = pl.ds(pl.multiple_of(core * half, half), half)
    side_half = pl.ds(pl.multiple_of((1 - core) * half, half), half)

    def attend_half(which, here):
        visible = visible_to(which)
        pieces = attention(query_v[here, :], key_v[...], value_v[...], visible)
        for index, piece in enumerate(pieces):
            text_context[here, pl.ds(index * 128, piece.shape[1])] = piece

    attend_half(1 - core, side_half)
    side = to_tp(text_context.at[side_half, :], text_got, last_s.at[0], last_r.at[0], sibling)
    side.start()
    attend_half(core, own_half)
    load_tout.wait()
    summed = matmul(text_context[own_half, :], tout_v[0])
    tout_copy.wait_recv()
    side.wait_recv()
    summed = (summed + matmul(text_got[...], tout_v[1])).astype(BF16)
    last_send[...] = summed
    last = to_tp(last_send, last_got, last_s.at[1], last_r.at[1], across)
    last.start()
    prompt_v[...] = put(table, covered, chosen_v[...].reshape(all_cells, -1), prompt_v[...])
    residual = prompt_v[own_half, :].astype(F32)
    last.wait_recv()
    total = summed.astype(F32) + last_got[...].astype(F32)
    out[own_half, :] = (residual + total).astype(BF16)
    done = to_tp(
        out.at[own_half, :], out.at[own_half, :], last_s.at[2], last_r.at[2], sibling
    )
    done.start()

    def sent(d):
        gather_copy(d + 1).wait_send()

    each(seq_count // 2 - 1, sent)

    def handed_on(d):
        relay_copy(d).wait_send()

    each(seq_count // 2, handed_on)
    for copy in [vout_copy, tout_copy, tok_across, cross, side, last]:
        copy.wait_send()
    for copy in half_copies + term_copies + chosen_copies:
        copy.wait_send()
    done.wait()


def local(
    seq_count,
    patches,
    picture_grid,
    vision_qkv,
    vision_out,
    merge_weight,
    picture_block,
    picture_offset,
    tokens,
    prompt_lengths,
    text_qkv,
    text_out,
):
    hops = (seq_count + 3) // 4
    blocks = hops + 1
    count, model = patches.shape[1:]
    rows, width = tokens.shape
    share, half = MERGED // 4, rows // 2
    dma = pltpu.SemaphoreType.DMA
    hbm = pl.BlockSpec(memory_space=pltpu.HBM)
    scalars = pl.BlockSpec(memory_space=pltpu.SMEM)
    vmem = pl.BlockSpec(memory_space=pltpu.VMEM)
    return pl.pallas_call(
        functools.partial(kernel, seq_count, hops),
        out_shape=pltpu.VMEM((rows, model), BF16),
        in_specs=[hbm, scalars, hbm, hbm, hbm, scalars, scalars, hbm, scalars, hbm, hbm],
        out_specs=vmem,
        scratch_shapes=[
            pltpu.VMEM((count, model), BF16),
            pltpu.VMEM((3, width, model), BF16),
            pltpu.VMEM((2, width, model), BF16),
            pltpu.VMEM((model, model), BF16),
            pltpu.VMEM((3, width, model), BF16),
            pltpu.VMEM((2, width, model), BF16),
            pltpu.VMEM((blocks, 4, width, rows), BF16),
            pltpu.VMEM((seq_count, 8, 128), jnp.int32),
            pltpu.VMEM((count, width), BF16),
            pltpu.VMEM((2, MERGED, width), BF16),
            pltpu.VMEM((MERGED, model), BF16),
            pltpu.VMEM((MERGED, model), BF16),
            pltpu.VMEM((MERGED, model), F32),
            pltpu.VMEM((4, share, model), BF16),
            pltpu.VMEM((4, share, model), BF16),
            pltpu.VMEM((seq_count, share, model), BF16),
            pltpu.VMEM((4, blocks * share, model), BF16),
            pltpu.VMEM((4, blocks * share, model), BF16),
            pltpu.VMEM((count, width), BF16),
            pltpu.VMEM((blocks * rows, model), BF16),
            pltpu.VMEM((rows, model), BF16),
            pltpu.VMEM((rows, width), BF16),
            pltpu.VMEM((blocks * rows, width), BF16),
            pltpu.VMEM((blocks * rows, width), BF16),
            pltpu.VMEM((rows, width), BF16),
            pltpu.VMEM((half, width), BF16),
            pltpu.VMEM((half, model), BF16),
            pltpu.VMEM((half, model), BF16),
            dma((7,)),
            dma((2,)),
            dma((2,)),
            dma((1,)),
            dma((1,)),
            dma((blocks, 2)),
            dma((blocks, 2)),
            dma((blocks, 2)),
            dma((blocks, 2)),
            dma((seq_count,)),
            dma((seq_count,)),
            dma((2,)),
            dma((2,)),
            dma((1,)),
            dma((1,)),
            dma((4,)),
            dma((4,)),
            dma((seq_count,)),
            dma((seq_count,)),
            dma((seq_count,)),
            dma((seq_count,)),
            dma((3,)),
            dma((3,)),
            dma((3,)),
            dma((3,)),
        ],
        compiler_params=pltpu.CompilerParams(
            collective_id=0, has_side_effects=True, vmem_limit_bytes=56 * 1024 * 1024
        ),
    )(
        patches,
        picture_grid,
        jnp.transpose(vision_qkv, (1, 2, 0)),
        vision_out,
        merge_weight,
        picture_block,
        picture_offset,
        tokens.T,
        prompt_lengths,
        jnp.transpose(text_qkv, (1, 2, 0)),
        text_out,
    )


def solution(mesh):
    placed = (
        P("seq", None, None),
        P("seq", None),
        P(None, None, "tp"),
        P("tp", None),
        P("tp", None, None),
        P("seq"),
        P("seq"),
        P("seq", "tp"),
        P(),
        P(None, None, "tp"),
        P("tp", None),
    )
    return jax.shard_map(
        functools.partial(local, mesh.shape["seq"]),
        mesh=mesh,
        in_specs=placed,
        out_specs=P("seq", None),
        check_vma=False,
    )
```

```python
import functools

import jax
import jax.numpy as jnp
from jax import lax
from jax.experimental import pallas as pl
from jax.experimental.pallas import tpu as pltpu
from jax.sharding import PartitionSpec as P

HEAD = 88
MAXGRID = 16
MERGED = 64
EPSILON = 1e-06
MASKED = -1e31
LOG2E = 1.4426950408889634
F32 = jnp.float32
BF16 = jnp.bfloat16


def normalize(values):
    values = values.astype(F32)
    centre = jnp.mean(values, axis=-1, keepdims=True)
    shifted = values - centre
    spread = jnp.mean(shifted * shifted, axis=-1, keepdims=True)
    return (shifted * lax.rsqrt(spread + EPSILON)).astype(BF16)


def matmul(a, b):
    return jnp.dot(a, b, preferred_element_type=F32)


def matmul_rows(a, b):
    return lax.dot_general(a, b, (((1,), (1,)), ((), ())), preferred_element_type=F32)


def attention(query, keys, values, allowed):
    width = query.shape[1]
    parts = [None] * (-(-width // 128))
    for head in range(width // HEAD):
        first, last = head * HEAD, (head + 1) * HEAD
        low, high = first // 128 * 128, min(width, -(-last // 128) * 128)
        lane = lax.broadcasted_iota(jnp.int32, (1, high - low), 1) + low
        inside = ((lane >= first) & (lane < last)).astype(F32).astype(BF16)
        scores = matmul_rows(query[:, low:high] * inside, keys[:, low:high])
        scores = jnp.where(allowed, scores, MASKED)
        top = jnp.max(scores, axis=-1, keepdims=True)
        expons = jnp.exp2((scores - top) * (HEAD ** (-0.5) * LOG2E))
        total = jnp.sum(expons, axis=-1, keepdims=True)
        context = matmul(expons.astype(BF16), values[:, low:high] * inside) * (1.0 / total)
        for at in range(low, high, 128):
            piece = context[:, at - low : min(high, at + 128) - low]
            slot = at // 128
            parts[slot] = piece if parts[slot] is None else parts[slot] + piece
    return [part.astype(BF16) for part in parts]


def each(count, body):
    if count <= 4:
        for index in range(count):
            body(index)
    else:

        def step(index, _):
            body(index)
            return 0

        lax.fori_loop(0, count, step, 0)


def kernel(
    seq_count,
    hops,
    patches,
    grid,
    vqkv,
    vout,
    merge,
    block,
    offset,
    tokens,
    lengths,
    tqkv,
    tout,
    out,
    patch_v,
    vqkv_v,
    vout_v,
    merge_v,
    tqkv_v,
    tout_v,
    tok_v,
    meta_v,
    context_v,
    context_got,
    cross_send,
    cross_got,
    term_v,
    term_send,
    term_got,
    gathered,
    chosen_v,
    cells_normed,
    patch_query,
    normed_v,
    prompt_v,
    query_v,
    key_v,
    value_v,
    text_context,
    text_got,
    last_send,
    last_got,
    load_sem,
    weight_s,
    weight_r,
    tok_across_s,
    tok_across_r,
    tok_seq_s,
    tok_seq_r,
    tok_side_s,
    tok_side_r,
    meta_s,
    meta_r,
    half_s,
    half_r,
    cross_s,
    cross_r,
    term_s,
    term_r,
    gather_s,
    gather_r,
    relay_s,
    relay_r,
    chosen_s,
    chosen_r,
    last_s,
    last_r,
):
    me = lax.axis_index("seq")
    t = lax.axis_index("tp")
    tp = 4
    rows = tokens.shape[1]
    blocks = hops + 1
    sibling = t + 1 - 2 * lax.rem(t, 2)
    across = lax.rem(t + 2, 4)
    opposite = 3 - t
    partner = me + 1 - 2 * lax.rem(me, 2)

    def load(source, target, index):
        copy = pltpu.make_async_copy(source, target, load_sem.at[index])
        copy.start()
        return copy

    def remote(source, target, send, recv, device):
        return pltpu.make_async_remote_copy(
            src_ref=source,
            dst_ref=target,
            send_sem=send,
            recv_sem=recv,
            device_id=device,
            device_id_type=pl.DeviceIdType.MESH,
        )

    def to_tp(source, target, send, recv, peer):
        return remote(source, target, send, recv, (me, peer))

    def to_seq(source, target, send, recv, peer):
        return remote(source, target, send, recv, (peer, t))

    load_patches = load(patches.at[0], patch_v, 0)
    load_vqkv = load(vqkv, vqkv_v, 1)

    barrier = pltpu.get_barrier_semaphore()
    for d in range(1, tp):
        pl.semaphore_signal(
            barrier, inc=1, device_id=(me, lax.rem(t + d, tp)), device_id_type=pl.DeviceIdType.MESH
        )

    def greet(d, _):
        pl.semaphore_signal(
            barrier,
            inc=1,
            device_id=(lax.rem(me + d, seq_count), t),
            device_id_type=pl.DeviceIdType.MESH,
        )
        return 0

    lax.fori_loop(1, seq_count, greet, 0)

    half_rows, half_cols = grid[0, 0], grid[0, 1]
    count = patch_v.shape[0]

    def ordering(first, size):
        slot = lax.broadcasted_iota(jnp.int32, (size, 1), 0) + first
        row = ((slot >> 3) & 7) * 2 + (slot >> 7)
        col = (slot & 7) * 2 + ((slot >> 6) & 1)
        picked = row * MAXGRID + col == lax.broadcasted_iota(jnp.int32, (size, count), 1)
        return picked.astype(F32).astype(BF16)

    order = ordering(0, count)
    key_slot = lax.broadcasted_iota(jnp.int32, (1, count), 1)
    key_allowed = (key_slot >> 4 < 2 * half_rows) & ((key_slot & 15) < 2 * half_cols)
    load_patches.wait()
    normed = normalize(patch_v[...])
    load_vqkv.wait()
    load_tokens = load(tokens, tok_v.at[0, t], 6)
    load_vout = load(vout, vout_v.at[0], 2)
    load_merge = load(merge.at[0], merge_v, 3)
    load_tqkv = load(tqkv, tqkv_v, 4)
    load_tout = load(tout, tout_v.at[0], 5)
    patch_query[...] = matmul(order, matmul_rows(normed, vqkv_v[0]).astype(BF16)).astype(BF16)
    keys = matmul_rows(normed, vqkv_v[1]).astype(BF16)
    values = matmul_rows(normed, vqkv_v[2]).astype(BF16)

    field = lax.broadcasted_iota(jnp.int32, (8, 128), 0)
    meta_v[me] = jnp.where(
        field == 0,
        half_rows,
        jnp.where(field == 1, half_cols, jnp.where(field == 2, block[0], offset[0])),
    )
    pl.semaphore_wait(barrier, tp - 1 + seq_count - 1)
    vout_copy = to_tp(vout, vout_v.at[1], weight_s.at[0], weight_r.at[0], sibling)
    vout_copy.start()
    tok_across = to_tp(tokens, tok_v.at[0, t], tok_across_s.at[0], tok_across_r.at[0], across)
    tok_across.start()

    def meta_copy(d):
        return to_seq(
            meta_v.at[me], meta_v.at[me], meta_s.at[d], meta_r.at[d], lax.rem(me + d, seq_count)
        )

    def send_meta(d, _):
        meta_copy(d).start()
        return 0

    lax.fori_loop(1, seq_count, send_meta, 0)

    def patch_rows(which):
        return pl.ds(pl.multiple_of(which * MERGED, MERGED), MERGED)

    def attend_patches(first, second):
        pair = (first, second)
        asking = jnp.concatenate([patch_query[patch_rows(which), :] for which in pair], axis=0)
        for index, piece in enumerate(attention(asking, keys, values, key_allowed)):
            lanes = pl.ds(index * 128, piece.shape[1])
            for place, which in enumerate(pair):
                context_v[patch_rows(which), lanes] = piece[place * MERGED : (place + 1) * MERGED]

    def share_context(index, which):
        copy = to_tp(
            context_v.at[patch_rows(which), :],
            context_got.at[index],
            half_s.at[index],
            half_r.at[index],
            sibling,
        )
        copy.start()
        return copy

    attend_patches(opposite, across)
    half_copies = [share_context(1, opposite)]
    load_vout.wait()
    far = matmul(context_v[patch_rows(across), :], vout_v[0])
    vout_copy.wait_recv()
    half_copies[0].wait_recv()
    cross_send[...] = (far + matmul(context_got[1], vout_v[1])).astype(BF16)
    cross = to_tp(cross_send, cross_got, cross_s.at[0], cross_r.at[0], across)
    cross.start()
    tout_copy = to_tp(tout, tout_v.at[1], weight_s.at[1], weight_r.at[1], sibling)
    tout_copy.start()
    load_tokens.wait()
    tok_across.wait_recv()

    def tok_seq_copy(hop, index):
        piece = t if index == 0 else across
        return to_seq(
            tok_v.at[0, piece],
            tok_v.at[hop, piece],
            tok_seq_s.at[hop, index],
            tok_seq_r.at[hop, index],
            lax.rem(me + hop, seq_count),
        )

    def tok_side_copy(hop, index):
        piece = t if index == 0 else across
        return to_tp(
            tok_v.at[hop, piece],
            tok_v.at[hop, piece],
            tok_side_s.at[hop, index],
            tok_side_r.at[hop, index],
            sibling,
        )

    def send_tokens(hop):
        for index in range(2):
            tok_seq_copy(hop + 1, index).start()

    each(hops, send_tokens)
    for index in range(2):
        tok_side_copy(0, index).start()

    attend_patches(sibling, t)
    half_copies.append(share_context(0, sibling))
    near = matmul(context_v[patch_rows(t), :], vout_v[0])
    half_copies[1].wait_recv()
    near = near + matmul(context_got[0], vout_v[1])
    hidden = matmul(ordering(t * MERGED, MERGED), patch_v[...]) + near

    load_merge.wait()
    cross.wait_recv()
    merged_in = normalize(hidden + cross_got[...].astype(F32))

    share = MERGED // tp
    term_v[...] = matmul(merged_in, merge_v[...])
    term_copies = []
    for d in (2, 3, 1):
        peer = lax.rem(t + d, tp)
        term_send[d] = term_v[pl.ds(pl.multiple_of(peer * share, share), share), :].astype(BF16)
        copy = to_tp(term_send.at[d], term_got.at[d], term_s.at[d], term_r.at[d], peer)
        copy.start()
        term_copies.append(copy)

    def side_tokens(hop):
        for index in range(2):
            tok_seq_copy(hop + 1, index).wait()
            tok_side_copy(hop + 1, index).start()

    def tokens_in(hop):
        for index in range(2):
            tok_side_copy(hop, index).wait()

    same = (
        lax.broadcasted_iota(jnp.int32, (rows, rows), 0)
        == lax.broadcasted_iota(jnp.int32, (rows, rows), 1)
    )
    same = same.astype(F32).astype(BF16)

    def block_rows(hop):
        return pl.ds(pl.multiple_of(hop * rows, rows), rows)

    def norm_tokens(hop):
        whole_rows = matmul_rows(same, tok_v[hop].reshape(-1, rows))
        normed_v[block_rows(hop), :] = normalize(whole_rows)
        return whole_rows

    tokens_in(0)
    prompt_v[...] = norm_tokens(0).astype(BF16)
    merged = term_v[pl.ds(pl.multiple_of(t * share, share), share), :]
    for copy, d in zip(term_copies, (2, 3, 1)):
        copy.wait_recv()
        merged = merged + term_got[d].astype(F32)
    gathered[me] = merged.astype(BF16)

    def gather_copy(d):
        return to_seq(
            gathered.at[me],
            gathered.at[me],
            gather_s.at[d],
            gather_r.at[d],
            lax.rem(me + 2 * d, seq_count),
        )

    def relay_copy(d):
        piece = lax.rem(me + seq_count - 2 * d, seq_count)
        return to_seq(
            gathered.at[piece], gathered.at[piece], relay_s.at[d], relay_r.at[d], partner
        )

    def send_merged(d):
        gather_copy(d + 1).start()

    each(seq_count // 2 - 1, send_merged)
    relay_copy(0).start()

    each(hops, side_tokens)
    load_tqkv.wait()
    query_v[...] = matmul_rows(normed_v[0:rows, :], tqkv_v[0]).astype(BF16)

    def relay(d):
        gather_copy(d + 1).wait_recv()
        relay_copy(d + 1).start()

    def norm_earlier(hop):
        tokens_in(hop + 1)
        norm_tokens(hop + 1)

    each(seq_count // 2 - 1, relay)
    each(hops, norm_earlier)
    group = 3 if blocks % 3 == 0 else 1

    def project(index):
        some = pl.ds(pl.multiple_of(index * group * rows, rows), group * rows)
        key_v[some, :] = matmul_rows(normed_v[some, :], tqkv_v[1]).astype(BF16)
        value_v[some, :] = matmul_rows(normed_v[some, :], tqkv_v[2]).astype(BF16)

    each(blocks // group, project)
    half = rows // 2
    core = lax.rem(t, 2)

    def visible_to(which):
        position = lax.broadcasted_iota(jnp.int32, (half, 1), 0) + me * rows + which * half
        start = jnp.zeros((half, 1), jnp.int32)
        end = jnp.int32(0)
        for index in range(lengths.shape[0]):
            end = end + lengths[index]
            start = jnp.where(end <= position, end, start)
        lane = lax.broadcasted_iota(jnp.int32, (1, blocks * rows), 1)
        key_position = (me - lane // rows) * rows + lane % rows
        return (key_position <= position) & (key_position >= start)

    def meta_arrived(d, _):
        meta_copy(d).wait()
        return 0

    lax.fori_loop(1, seq_count, meta_arrived, 0)

    def relayed(d):
        relay_copy(d).wait_recv()

    each(seq_count // 2, relayed)

    def choose(hop):
        def add(index, cells_sum):
            hit = (meta_v[index][2:3, 0:1] == me - hop).astype(F32)
            return cells_sum + gathered[index].astype(F32) * hit

        cells_sum = jnp.zeros((share, patch_v.shape[1]), F32)
        if seq_count <= 8:
            for index in range(seq_count):
                cells_sum = add(index, cells_sum)
        else:
            cells_sum = lax.fori_loop(0, seq_count, add, cells_sum)
        chosen_v[t, pl.ds(pl.multiple_of(hop * share, share), share), :] = cells_sum.astype(BF16)

    each(blocks, choose)

    def chosen_copy(index, piece, peer):
        return to_tp(
            chosen_v.at[piece], chosen_v.at[piece], chosen_s.at[index], chosen_r.at[index], peer
        )

    chosen_copies = [chosen_copy(0, t, across), chosen_copy(1, t, sibling)]
    for copy in chosen_copies:
        copy.start()

    all_cells = blocks * MERGED
    lane = lax.broadcasted_iota(jnp.int32, (1, all_cells), 1)
    lane_hop = lane % (blocks * share) // share
    lane_cell = lane // (blocks * share) * share + lane % share
    row_cell, col_cell = lane_cell // 8, lane_cell % 8

    def placement(hop):
        def add(index, state):
            about, present = state
            hit = (meta_v[index][2:3, :] == me - hop).astype(jnp.int32)
            return about + meta_v[index] * hit, present + hit

        about, present = lax.fori_loop(
            0, seq_count, add, (jnp.zeros((8, 128), jnp.int32), jnp.zeros((1, 128), jnp.int32))
        )
        g0, g1 = about[0:1, 0:1], about[1:2, 0:1]
        usable = (row_cell < g0) & (col_cell < g1) & (present[:, 0:1] > 0) & (lane_hop == hop)
        target = jnp.where(usable, about[3:4, 0:1] + row_cell * g1 + col_cell, -1)
        table = (lax.broadcasted_iota(jnp.int32, (rows, all_cells), 0) == target).astype(F32)
        return table.astype(BF16), jnp.max(table, axis=1, keepdims=True)

    if blocks <= 4:
        placements = [placement(hop) for hop in range(blocks)]

    def placement_of(hop):
        return placements[hop] if blocks <= 4 else placement(hop)

    cells_normed[t] = normalize(chosen_v[t])
    chosen_copies[1].wait_recv()
    cells_normed[sibling] = normalize(chosen_v[sibling])
    chosen_copies[0].wait_recv()
    chosen_copies.append(chosen_copy(2, across, sibling))
    chosen_copies[2].start()
    cells_normed[across] = normalize(chosen_v[across])
    chosen_copies[2].wait_recv()
    cells_normed[opposite] = normalize(chosen_v[opposite])
    normed = cells_normed[...].reshape(all_cells, -1)
    query_cells = matmul_rows(normed, tqkv_v[0]).astype(BF16)
    key_cells = matmul_rows(normed, tqkv_v[1]).astype(BF16)
    value_cells = matmul_rows(normed, tqkv_v[2]).astype(BF16)

    def put(table, covered, cells_here, before):
        return jnp.where(
            covered > 0, matmul(table, cells_here), before.astype(F32)
        ).astype(BF16)

    def put_block(hop):
        table, covered = placement_of(hop)
        here = block_rows(hop)
        key_v[here, :] = put(table, covered, key_cells, key_v[here, :])
        value_v[here, :] = put(table, covered, value_cells, value_v[here, :])

    each(blocks, put_block)
    table, covered = placement_of(0)
    query_v[...] = put(table, covered, query_cells, query_v[...])

    own_half = pl.ds(pl.multiple_of(core * half, half), half)
    side_half = pl.ds(pl.multiple_of((1 - core) * half, half), half)

    def attend_half(which, here):
        visible = visible_to(which)
        pieces = attention(query_v[here, :], key_v[...], value_v[...], visible)
        for index, piece in enumerate(pieces):
            text_context[here, pl.ds(index * 128, piece.shape[1])] = piece

    attend_half(1 - core, side_half)
    side = to_tp(text_context.at[side_half, :], text_got, last_s.at[0], last_r.at[0], sibling)
    side.start()
    attend_half(core, own_half)
    load_tout.wait()
    summed = matmul(text_context[own_half, :], tout_v[0])
    tout_copy.wait_recv()
    side.wait_recv()
    summed = (summed + matmul(text_got[...], tout_v[1])).astype(BF16)
    last_send[...] = summed
    last = to_tp(last_send, last_got, last_s.at[1], last_r.at[1], across)
    last.start()
    prompt_v[...] = put(table, covered, chosen_v[...].reshape(all_cells, -1), prompt_v[...])
    residual = prompt_v[own_half, :].astype(F32)
    last.wait_recv()
    total = summed.astype(F32) + last_got[...].astype(F32)
    out[own_half, :] = (residual + total).astype(BF16)
    done = to_tp(
        out.at[own_half, :], out.at[own_half, :], last_s.at[2], last_r.at[2], sibling
    )
    done.start()

    def sent(d):
        gather_copy(d + 1).wait_send()

    each(seq_count // 2 - 1, sent)

    def handed_on(d):
        relay_copy(d).wait_send()

    each(seq_count // 2, handed_on)
    for copy in [vout_copy, tout_copy, tok_across, cross, side, last]:
        copy.wait_send()
    for copy in half_copies + term_copies + chosen_copies:
        copy.wait_send()
    done.wait()


def local(
    seq_count,
    patches,
    picture_grid,
    vision_qkv,
    vision_out,
    merge_weight,
    picture_block,
    picture_offset,
    tokens,
    prompt_lengths,
    text_qkv,
    text_out,
):
    hops = (seq_count + 3) // 4
    blocks = hops + 1
    count, model = patches.shape[1:]
    rows, width = tokens.shape
    share, half = MERGED // 4, rows // 2
    dma = pltpu.SemaphoreType.DMA
    hbm = pl.BlockSpec(memory_space=pltpu.HBM)
    scalars = pl.BlockSpec(memory_space=pltpu.SMEM)
    vmem = pl.BlockSpec(memory_space=pltpu.VMEM)
    return pl.pallas_call(
        functools.partial(kernel, seq_count, hops),
        out_shape=pltpu.VMEM((rows, model), BF16),
        in_specs=[hbm, scalars, hbm, hbm, hbm, scalars, scalars, hbm, scalars, hbm, hbm],
        out_specs=vmem,
        scratch_shapes=[
            pltpu.VMEM((count, model), BF16),
            pltpu.VMEM((3, width, model), BF16),
            pltpu.VMEM((2, width, model), BF16),
            pltpu.VMEM((model, model), BF16),
            pltpu.VMEM((3, width, model), BF16),
            pltpu.VMEM((2, width, model), BF16),
            pltpu.VMEM((blocks, 4, width, rows), BF16),
            pltpu.VMEM((seq_count, 8, 128), jnp.int32),
            pltpu.VMEM((count, width), BF16),
            pltpu.VMEM((2, MERGED, width), BF16),
            pltpu.VMEM((MERGED, model), BF16),
            pltpu.VMEM((MERGED, model), BF16),
            pltpu.VMEM((MERGED, model), F32),
            pltpu.VMEM((4, share, model), BF16),
            pltpu.VMEM((4, share, model), BF16),
            pltpu.VMEM((seq_count, share, model), BF16),
            pltpu.VMEM((4, blocks * share, model), BF16),
            pltpu.VMEM((4, blocks * share, model), BF16),
            pltpu.VMEM((count, width), BF16),
            pltpu.VMEM((blocks * rows, model), BF16),
            pltpu.VMEM((rows, model), BF16),
            pltpu.VMEM((rows, width), BF16),
            pltpu.VMEM((blocks * rows, width), BF16),
            pltpu.VMEM((blocks * rows, width), BF16),
            pltpu.VMEM((rows, width), BF16),
            pltpu.VMEM((half, width), BF16),
            pltpu.VMEM((half, model), BF16),
            pltpu.VMEM((half, model), BF16),
            dma((7,)),
            dma((2,)),
            dma((2,)),
            dma((1,)),
            dma((1,)),
            dma((blocks, 2)),
            dma((blocks, 2)),
            dma((blocks, 2)),
            dma((blocks, 2)),
            dma((seq_count,)),
            dma((seq_count,)),
            dma((2,)),
            dma((2,)),
            dma((1,)),
            dma((1,)),
            dma((4,)),
            dma((4,)),
            dma((seq_count,)),
            dma((seq_count,)),
            dma((seq_count,)),
            dma((seq_count,)),
            dma((3,)),
            dma((3,)),
            dma((3,)),
            dma((3,)),
        ],
        compiler_params=pltpu.CompilerParams(
            collective_id=0, has_side_effects=True, vmem_limit_bytes=56 * 1024 * 1024
        ),
    )(
        patches,
        picture_grid,
        jnp.transpose(vision_qkv, (1, 2, 0)),
        vision_out,
        merge_weight,
        picture_block,
        picture_offset,
        tokens.T,
        prompt_lengths,
        jnp.transpose(text_qkv, (1, 2, 0)),
        text_out,
    )


def solution(mesh):
    placed = (
        P("seq", None, None),
        P("seq", None),
        P(None, None, "tp"),
        P("tp", None),
        P("tp", None, None),
        P("seq"),
        P("seq"),
        P("seq", "tp"),
        P(),
        P(None, None, "tp"),
        P("tp", None),
    )
    return jax.shard_map(
        functools.partial(local, mesh.shape["seq"]),
        mesh=mesh,
        in_specs=placed,
        out_specs=P("seq", None),
        check_vma=False,
    )
```

```python
import functools

import jax
import jax.numpy as jnp
from jax import lax
from jax.experimental import pallas as pl
from jax.experimental.pallas import tpu as pltpu
from jax.sharding import PartitionSpec as P

HEAD = 88
MAXGRID = 16
MERGED = 64
EPSILON = 1e-06
MASKED = -1e31
LOG2E = 1.4426950408889634
F32 = jnp.float32
BF16 = jnp.bfloat16


def normalize(values):
    values = values.astype(F32)
    centre = jnp.mean(values, axis=-1, keepdims=True)
    shifted = values - centre
    spread = jnp.mean(shifted * shifted, axis=-1, keepdims=True)
    return (shifted * lax.rsqrt(spread + EPSILON)).astype(BF16)


def matmul(a, b):
    return jnp.dot(a, b, preferred_element_type=F32)


def matmul_rows(a, b):
    return lax.dot_general(a, b, (((1,), (1,)), ((), ())), preferred_element_type=F32)


def attention(query, keys, values, allowed):
    width = query.shape[1]
    parts = [None] * (-(-width // 128))
    for head in range(width // HEAD):
        first, last = head * HEAD, (head + 1) * HEAD
        low, high = first // 128 * 128, min(width, -(-last // 128) * 128)
        lane = lax.broadcasted_iota(jnp.int32, (1, high - low), 1) + low
        inside = ((lane >= first) & (lane < last)).astype(F32).astype(BF16)
        scores = matmul_rows(query[:, low:high] * inside, keys[:, low:high])
        scores = jnp.where(allowed, scores, MASKED)
        top = jnp.max(scores, axis=-1, keepdims=True)
        expons = jnp.exp2((scores - top) * (HEAD ** (-0.5) * LOG2E))
        total = jnp.sum(expons, axis=-1, keepdims=True)
        context = matmul(expons.astype(BF16), values[:, low:high] * inside) * (1.0 / total)
        for at in range(low, high, 128):
            piece = context[:, at - low : min(high, at + 128) - low]
            slot = at // 128
            parts[slot] = piece if parts[slot] is None else parts[slot] + piece
    return [part.astype(BF16) for part in parts]


def each(count, body):
    if count <= 4:
        for index in range(count):
            body(index)
    else:

        def step(index, _):
            body(index)
            return 0

        lax.fori_loop(0, count, step, 0)


def kernel(
    seq_count,
    hops,
    patches,
    grid,
    vqkv,
    vout,
    merge,
    block,
    offset,
    tokens,
    lengths,
    tqkv,
    tout,
    out,
    patch_v,
    vqkv_v,
    vout_v,
    merge_v,
    tqkv_v,
    tout_v,
    tok_v,
    meta_v,
    context_v,
    half_send,
    half_got,
    cross_send,
    cross_got,
    term_v,
    term_send,
    term_got,
    gathered,
    chosen_v,
    cells_normed,
    patch_query,
    normed_v,
    prompt_v,
    query_v,
    key_v,
    value_v,
    text_context,
    text_got,
    last_send,
    last_got,
    load_sem,
    weight_s,
    weight_r,
    tok_across_s,
    tok_across_r,
    tok_seq_s,
    tok_seq_r,
    tok_side_s,
    tok_side_r,
    meta_s,
    meta_r,
    half_s,
    half_r,
    cross_s,
    cross_r,
    term_s,
    term_r,
    gather_s,
    gather_r,
    relay_s,
    relay_r,
    chosen_s,
    chosen_r,
    last_s,
    last_r,
):
    me = lax.axis_index("seq")
    t = lax.axis_index("tp")
    tp = 4
    rows = tokens.shape[1]
    blocks = hops + 1
    sibling = t + 1 - 2 * lax.rem(t, 2)
    across = lax.rem(t + 2, 4)
    opposite = 3 - t
    partner = me + 1 - 2 * lax.rem(me, 2)

    def load(source, target, index):
        copy = pltpu.make_async_copy(source, target, load_sem.at[index])
        copy.start()
        return copy

    def remote(source, target, send, recv, device):
        return pltpu.make_async_remote_copy(
            src_ref=source,
            dst_ref=target,
            send_sem=send,
            recv_sem=recv,
            device_id=device,
            device_id_type=pl.DeviceIdType.MESH,
        )

    def to_tp(source, target, send, recv, peer):
        return remote(source, target, send, recv, (me, peer))

    def to_seq(source, target, send, recv, peer):
        return remote(source, target, send, recv, (peer, t))

    load_patches = load(patches.at[0], patch_v, 0)
    load_vqkv = load(vqkv, vqkv_v, 1)

    barrier = pltpu.get_barrier_semaphore()
    for d in range(1, tp):
        pl.semaphore_signal(
            barrier, inc=1, device_id=(me, lax.rem(t + d, tp)), device_id_type=pl.DeviceIdType.MESH
        )

    def greet(d, _):
        pl.semaphore_signal(
            barrier,
            inc=1,
            device_id=(lax.rem(me + d, seq_count), t),
            device_id_type=pl.DeviceIdType.MESH,
        )
        return 0

    lax.fori_loop(1, seq_count, greet, 0)

    half_rows, half_cols = grid[0, 0], grid[0, 1]
    count = patch_v.shape[0]

    def ordering(first, size):
        slot = lax.broadcasted_iota(jnp.int32, (size, 1), 0) + first
        row = ((slot >> 3) & 7) * 2 + (slot >> 7)
        col = (slot & 7) * 2 + ((slot >> 6) & 1)
        picked = row * MAXGRID + col == lax.broadcasted_iota(jnp.int32, (size, count), 1)
        return picked.astype(F32).astype(BF16)

    order = ordering(0, count)
    key_slot = lax.broadcasted_iota(jnp.int32, (1, count), 1)
    key_allowed = (key_slot >> 4 < 2 * half_rows) & ((key_slot & 15) < 2 * half_cols)
    load_patches.wait()
    normed = normalize(patch_v[...])
    load_vqkv.wait()
    load_tokens = load(tokens, tok_v.at[0, t], 6)
    load_vout = load(vout, vout_v, 2)
    load_merge = load(merge.at[0], merge_v, 3)
    load_tqkv = load(tqkv, tqkv_v, 4)
    load_tout = load(tout, tout_v.at[0], 5)
    patch_query[...] = matmul(order, matmul_rows(normed, vqkv_v[0]).astype(BF16)).astype(BF16)
    keys = matmul_rows(normed, vqkv_v[1]).astype(BF16)
    values = matmul_rows(normed, vqkv_v[2]).astype(BF16)

    field = lax.broadcasted_iota(jnp.int32, (8, 128), 0)
    meta_v[me] = jnp.where(
        field == 0,
        half_rows,
        jnp.where(field == 1, half_cols, jnp.where(field == 2, block[0], offset[0])),
    )
    pl.semaphore_wait(barrier, tp - 1 + seq_count - 1)
    tok_across = to_tp(tokens, tok_v.at[0, t], tok_across_s.at[0], tok_across_r.at[0], across)
    tok_across.start()

    def meta_copy(d):
        return to_seq(
            meta_v.at[me], meta_v.at[me], meta_s.at[d], meta_r.at[d], lax.rem(me + d, seq_count)
        )

    def send_meta(d, _):
        meta_copy(d).start()
        return 0

    lax.fori_loop(1, seq_count, send_meta, 0)

    def patch_rows(which):
        return pl.ds(pl.multiple_of(which * MERGED, MERGED), MERGED)

    def attend_patches(first, second):
        pair = (first, second)
        asking = jnp.concatenate([patch_query[patch_rows(which), :] for which in pair], axis=0)
        for index, piece in enumerate(attention(asking, keys, values, key_allowed)):
            lanes = pl.ds(index * 128, piece.shape[1])
            for place, which in enumerate(pair):
                context_v[patch_rows(which), lanes] = piece[place * MERGED : (place + 1) * MERGED]

    def partial_rows(which):
        return matmul(context_v[patch_rows(which), :], vout_v[...])

    def share_partial(index, which):
        half_send[index] = partial_rows(which).astype(BF16)
        copy = to_tp(
            half_send.at[index], half_got.at[index], half_s.at[index], half_r.at[index], sibling
        )
        copy.start()
        return copy

    attend_patches(opposite, across)
    load_vout.wait()
    half_copies = [share_partial(1, opposite)]
    far = partial_rows(across)
    half_copies[0].wait_recv()
    cross_send[...] = (far + half_got[1].astype(F32)).astype(BF16)
    cross = to_tp(cross_send, cross_got, cross_s.at[0], cross_r.at[0], across)
    cross.start()
    load_tokens.wait()
    tok_across.wait_recv()

    def tok_seq_copy(hop, index):
        piece = t if index == 0 else across
        return to_seq(
            tok_v.at[0, piece],
            tok_v.at[hop, piece],
            tok_seq_s.at[hop, index],
            tok_seq_r.at[hop, index],
            lax.rem(me + hop, seq_count),
        )

    def tok_side_copy(hop, index):
        piece = t if index == 0 else across
        return to_tp(
            tok_v.at[hop, piece],
            tok_v.at[hop, piece],
            tok_side_s.at[hop, index],
            tok_side_r.at[hop, index],
            sibling,
        )

    def send_tokens(hop):
        for index in range(2):
            tok_seq_copy(hop + 1, index).start()

    each(hops, send_tokens)
    for index in range(2):
        tok_side_copy(0, index).start()

    attend_patches(sibling, t)
    half_copies.append(share_partial(0, sibling))
    near = partial_rows(t)
    half_copies[1].wait_recv()
    near = near + half_got[0].astype(F32)
    hidden = matmul(ordering(t * MERGED, MERGED), patch_v[...]) + near

    load_merge.wait()
    cross.wait_recv()
    merged_in = normalize(hidden + cross_got[...].astype(F32))

    share = MERGED // tp
    term_v[...] = matmul(merged_in, merge_v[...])
    term_copies = []
    for d in (2, 3, 1):
        peer = lax.rem(t + d, tp)
        term_send[d] = term_v[pl.ds(pl.multiple_of(peer * share, share), share), :].astype(BF16)
        copy = to_tp(term_send.at[d], term_got.at[d], term_s.at[d], term_r.at[d], peer)
        copy.start()
        term_copies.append(copy)

    def side_tokens(hop):
        for index in range(2):
            tok_seq_copy(hop + 1, index).wait()
            tok_side_copy(hop + 1, index).start()

    def tokens_in(hop):
        for index in range(2):
            tok_side_copy(hop, index).wait()

    same = (
        lax.broadcasted_iota(jnp.int32, (rows, rows), 0)
        == lax.broadcasted_iota(jnp.int32, (rows, rows), 1)
    )
    same = same.astype(F32).astype(BF16)

    def block_rows(hop):
        return pl.ds(pl.multiple_of(hop * rows, rows), rows)

    def norm_tokens(hop):
        whole_rows = matmul_rows(same, tok_v[hop].reshape(-1, rows))
        normed_v[block_rows(hop), :] = normalize(whole_rows)
        return whole_rows

    tokens_in(0)
    prompt_v[...] = norm_tokens(0).astype(BF16)
    merged = term_v[pl.ds(pl.multiple_of(t * share, share), share), :]
    for copy, d in zip(term_copies, (2, 3, 1)):
        copy.wait_recv()
        merged = merged + term_got[d].astype(F32)
    gathered[me] = merged.astype(BF16)

    def gather_copy(d):
        return to_seq(
            gathered.at[me],
            gathered.at[me],
            gather_s.at[d],
            gather_r.at[d],
            lax.rem(me + 2 * d, seq_count),
        )

    def relay_copy(d):
        piece = lax.rem(me + seq_count - 2 * d, seq_count)
        return to_seq(
            gathered.at[piece], gathered.at[piece], relay_s.at[d], relay_r.at[d], partner
        )

    def send_merged(d):
        gather_copy(d + 1).start()

    each(seq_count // 2 - 1, send_merged)
    relay_copy(0).start()
    tout_copy = to_tp(tout, tout_v.at[1], weight_s.at[0], weight_r.at[0], sibling)
    tout_copy.start()

    each(hops, side_tokens)
    load_tqkv.wait()
    query_v[...] = matmul_rows(normed_v[0:rows, :], tqkv_v[0]).astype(BF16)

    def relay(d):
        gather_copy(d + 1).wait_recv()
        relay_copy(d + 1).start()

    def norm_earlier(hop):
        tokens_in(hop + 1)
        norm_tokens(hop + 1)

    each(seq_count // 2 - 1, relay)
    each(hops, norm_earlier)
    group = 3 if blocks % 3 == 0 else 1

    def project(index):
        some = pl.ds(pl.multiple_of(index * group * rows, rows), group * rows)
        key_v[some, :] = matmul_rows(normed_v[some, :], tqkv_v[1]).astype(BF16)
        value_v[some, :] = matmul_rows(normed_v[some, :], tqkv_v[2]).astype(BF16)

    each(blocks // group, project)
    half = rows // 2
    core = lax.rem(t, 2)

    def visible_to(which):
        position = lax.broadcasted_iota(jnp.int32, (half, 1), 0) + me * rows + which * half
        start = jnp.zeros((half, 1), jnp.int32)
        end = jnp.int32(0)
        for index in range(lengths.shape[0]):
            end = end + lengths[index]
            start = jnp.where(end <= position, end, start)
        lane = lax.broadcasted_iota(jnp.int32, (1, blocks * rows), 1)
        key_position = (me - lane // rows) * rows + lane % rows
        return (key_position <= position) & (key_position >= start)

    def meta_arrived(d, _):
        meta_copy(d).wait()
        return 0

    lax.fori_loop(1, seq_count, meta_arrived, 0)

    def relayed(d):
        relay_copy(d).wait_recv()

    each(seq_count // 2, relayed)

    def choose(hop):
        def add(index, cells_sum):
            hit = (meta_v[index][2:3, 0:1] == me - hop).astype(F32)
            return cells_sum + gathered[index].astype(F32) * hit

        cells_sum = jnp.zeros((share, patch_v.shape[1]), F32)
        if seq_count <= 8:
            for index in range(seq_count):
                cells_sum = add(index, cells_sum)
        else:
            cells_sum = lax.fori_loop(0, seq_count, add, cells_sum)
        chosen_v[t, pl.ds(pl.multiple_of(hop * share, share), share), :] = cells_sum.astype(BF16)

    each(blocks, choose)

    def chosen_copy(index, piece, peer):
        return to_tp(
            chosen_v.at[piece], chosen_v.at[piece], chosen_s.at[index], chosen_r.at[index], peer
        )

    chosen_copies = [chosen_copy(0, t, across), chosen_copy(1, t, sibling)]
    for copy in chosen_copies:
        copy.start()

    all_cells = blocks * MERGED
    lane = lax.broadcasted_iota(jnp.int32, (1, all_cells), 1)
    lane_hop = lane % (blocks * share) // share
    lane_cell = lane // (blocks * share) * share + lane % share
    row_cell, col_cell = lane_cell // 8, lane_cell % 8

    def placement(hop):
        def add(index, state):
            about, present = state
            hit = (meta_v[index][2:3, :] == me - hop).astype(jnp.int32)
            return about + meta_v[index] * hit, present + hit

        about, present = lax.fori_loop(
            0, seq_count, add, (jnp.zeros((8, 128), jnp.int32), jnp.zeros((1, 128), jnp.int32))
        )
        g0, g1 = about[0:1, 0:1], about[1:2, 0:1]
        usable = (row_cell < g0) & (col_cell < g1) & (present[:, 0:1] > 0) & (lane_hop == hop)
        target = jnp.where(usable, about[3:4, 0:1] + row_cell * g1 + col_cell, -1)
        table = (lax.broadcasted_iota(jnp.int32, (rows, all_cells), 0) == target).astype(F32)
        return table.astype(BF16), jnp.max(table, axis=1, keepdims=True)

    if blocks <= 4:
        placements = [placement(hop) for hop in range(blocks)]

    def placement_of(hop):
        return placements[hop] if blocks <= 4 else placement(hop)

    cells_normed[t] = normalize(chosen_v[t])
    chosen_copies[1].wait_recv()
    cells_normed[sibling] = normalize(chosen_v[sibling])
    chosen_copies[0].wait_recv()
    chosen_copies.append(chosen_copy(2, across, sibling))
    chosen_copies[2].start()
    cells_normed[across] = normalize(chosen_v[across])
    chosen_copies[2].wait_recv()
    cells_normed[opposite] = normalize(chosen_v[opposite])
    normed = cells_normed[...].reshape(all_cells, -1)
    query_cells = matmul_rows(normed, tqkv_v[0]).astype(BF16)
    key_cells = matmul_rows(normed, tqkv_v[1]).astype(BF16)
    value_cells = matmul_rows(normed, tqkv_v[2]).astype(BF16)

    def put(table, covered, cells_here, before):
        return jnp.where(
            covered > 0, matmul(table, cells_here), before.astype(F32)
        ).astype(BF16)

    def put_block(hop):
        table, covered = placement_of(hop)
        here = block_rows(hop)
        key_v[here, :] = put(table, covered, key_cells, key_v[here, :])
        value_v[here, :] = put(table, covered, value_cells, value_v[here, :])

    each(blocks, put_block)
    table, covered = placement_of(0)
    query_v[...] = put(table, covered, query_cells, query_v[...])

    own_half = pl.ds(pl.multiple_of(core * half, half), half)
    side_half = pl.ds(pl.multiple_of((1 - core) * half, half), half)

    def attend_half(which, here):
        visible = visible_to(which)
        pieces = attention(query_v[here, :], key_v[...], value_v[...], visible)
        for index, piece in enumerate(pieces):
            text_context[here, pl.ds(index * 128, piece.shape[1])] = piece

    attend_half(1 - core, side_half)
    side = to_tp(text_context.at[side_half, :], text_got, last_s.at[0], last_r.at[0], sibling)
    side.start()
    attend_half(core, own_half)
    load_tout.wait()
    summed = matmul(text_context[own_half, :], tout_v[0])
    tout_copy.wait_recv()
    side.wait_recv()
    summed = (summed + matmul(text_got[...], tout_v[1])).astype(BF16)
    last_send[...] = summed
    last = to_tp(last_send, last_got, last_s.at[1], last_r.at[1], across)
    last.start()
    prompt_v[...] = put(table, covered, chosen_v[...].reshape(all_cells, -1), prompt_v[...])
    residual = prompt_v[own_half, :].astype(F32)
    last.wait_recv()
    total = summed.astype(F32) + last_got[...].astype(F32)
    out[own_half, :] = (residual + total).astype(BF16)
    done = to_tp(
        out.at[own_half, :], out.at[own_half, :], last_s.at[2], last_r.at[2], sibling
    )
    done.start()

    def sent(d):
        gather_copy(d + 1).wait_send()

    each(seq_count // 2 - 1, sent)

    def handed_on(d):
        relay_copy(d).wait_send()

    each(seq_count // 2, handed_on)
    for copy in [tout_copy, tok_across, cross, side, last]:
        copy.wait_send()
    for copy in half_copies + term_copies + chosen_copies:
        copy.wait_send()
    done.wait()


def local(
    seq_count,
    patches,
    picture_grid,
    vision_qkv,
    vision_out,
    merge_weight,
    picture_block,
    picture_offset,
    tokens,
    prompt_lengths,
    text_qkv,
    text_out,
):
    hops = (seq_count + 3) // 4
    blocks = hops + 1
    count, model = patches.shape[1:]
    rows, width = tokens.shape
    share, half = MERGED // 4, rows // 2
    dma = pltpu.SemaphoreType.DMA
    hbm = pl.BlockSpec(memory_space=pltpu.HBM)
    scalars = pl.BlockSpec(memory_space=pltpu.SMEM)
    vmem = pl.BlockSpec(memory_space=pltpu.VMEM)
    return pl.pallas_call(
        functools.partial(kernel, seq_count, hops),
        out_shape=pltpu.VMEM((rows, model), BF16),
        in_specs=[hbm, scalars, hbm, hbm, hbm, scalars, scalars, hbm, scalars, hbm, hbm],
        out_specs=vmem,
        scratch_shapes=[
            pltpu.VMEM((count, model), BF16),
            pltpu.VMEM((3, width, model), BF16),
            pltpu.VMEM((width, model), BF16),
            pltpu.VMEM((model, model), BF16),
            pltpu.VMEM((3, width, model), BF16),
            pltpu.VMEM((2, width, model), BF16),
            pltpu.VMEM((blocks, 4, width, rows), BF16),
            pltpu.VMEM((seq_count, 8, 128), jnp.int32),
            pltpu.VMEM((count, width), BF16),
            pltpu.VMEM((2, MERGED, model), BF16),
            pltpu.VMEM((2, MERGED, model), BF16),
            pltpu.VMEM((MERGED, model), BF16),
            pltpu.VMEM((MERGED, model), BF16),
            pltpu.VMEM((MERGED, model), F32),
            pltpu.VMEM((4, share, model), BF16),
            pltpu.VMEM((4, share, model), BF16),
            pltpu.VMEM((seq_count, share, model), BF16),
            pltpu.VMEM((4, blocks * share, model), BF16),
            pltpu.VMEM((4, blocks * share, model), BF16),
            pltpu.VMEM((count, width), BF16),
            pltpu.VMEM((blocks * rows, model), BF16),
            pltpu.VMEM((rows, model), BF16),
            pltpu.VMEM((rows, width), BF16),
            pltpu.VMEM((blocks * rows, width), BF16),
            pltpu.VMEM((blocks * rows, width), BF16),
            pltpu.VMEM((rows, width), BF16),
            pltpu.VMEM((half, width), BF16),
            pltpu.VMEM((half, model), BF16),
            pltpu.VMEM((half, model), BF16),
            dma((7,)),
            dma((1,)),
            dma((1,)),
            dma((1,)),
            dma((1,)),
            dma((blocks, 2)),
            dma((blocks, 2)),
            dma((blocks, 2)),
            dma((blocks, 2)),
            dma((seq_count,)),
            dma((seq_count,)),
            dma((2,)),
            dma((2,)),
            dma((1,)),
            dma((1,)),
            dma((4,)),
            dma((4,)),
            dma((seq_count,)),
            dma((seq_count,)),
            dma((seq_count,)),
            dma((seq_count,)),
            dma((3,)),
            dma((3,)),
            dma((3,)),
            dma((3,)),
        ],
        compiler_params=pltpu.CompilerParams(
            collective_id=0, has_side_effects=True, vmem_limit_bytes=56 * 1024 * 1024
        ),
    )(
        patches,
        picture_grid,
        jnp.transpose(vision_qkv, (1, 2, 0)),
        vision_out,
        merge_weight,
        picture_block,
        picture_offset,
        tokens.T,
        prompt_lengths,
        jnp.transpose(text_qkv, (1, 2, 0)),
        text_out,
    )


def solution(mesh):
    placed = (
        P("seq", None, None),
        P("seq", None),
        P(None, None, "tp"),
        P("tp", None),
        P("tp", None, None),
        P("seq"),
        P("seq"),
        P("seq", "tp"),
        P(),
        P(None, None, "tp"),
        P("tp", None),
    )
    return jax.shard_map(
        functools.partial(local, mesh.shape["seq"]),
        mesh=mesh,
        in_specs=placed,
        out_specs=P("seq", None),
        check_vma=False,
    )
```

```python
import functools

import jax
import jax.numpy as jnp
from jax import lax
from jax.experimental import pallas as pl
from jax.experimental.pallas import tpu as pltpu
from jax.sharding import PartitionSpec as P

HEAD = 88
MAXGRID = 16
MERGED = 64
EPSILON = 1e-06
MASKED = -1e30
F32 = jnp.float32
BF16 = jnp.bfloat16


def normalize(values):
    values = values.astype(F32)
    centre = jnp.mean(values, axis=-1, keepdims=True)
    shifted = values - centre
    spread = jnp.mean(shifted * shifted, axis=-1, keepdims=True)
    return (shifted * lax.rsqrt(spread + EPSILON)).astype(BF16)


def matmul(a, b):
    return jnp.dot(a, b, preferred_element_type=F32)


def matmul_rows(a, b):
    return lax.dot_general(a, b, (((1,), (1,)), ((), ())), preferred_element_type=F32)


def attention(query, keys, values, allowed):
    width = query.shape[1]
    parts = [None] * (-(-width // 128))
    for head in range(width // HEAD):
        first, last = head * HEAD, (head + 1) * HEAD
        low, high = first // 128 * 128, min(width, -(-last // 128) * 128)
        lane = lax.broadcasted_iota(jnp.int32, (1, high - low), 1) + low
        inside = (lane >= first) & (lane < last)
        own_query = jnp.where(inside, query[:, low:high].astype(F32), 0.0).astype(BF16)
        own_values = jnp.where(inside, values[:, low:high].astype(F32), 0.0).astype(BF16)
        scores = matmul_rows(own_query, keys[:, low:high])
        scores = jnp.where(allowed, scores * HEAD ** (-0.5), MASKED)
        expons = jnp.exp(scores - jnp.max(scores, axis=-1, keepdims=True))
        total = jnp.sum(expons, axis=-1, keepdims=True)
        context = matmul(expons.astype(BF16), own_values) / total
        for at in range(low, high, 128):
            piece = context[:, at - low : min(high, at + 128) - low]
            slot = at // 128
            parts[slot] = piece if parts[slot] is None else parts[slot] + piece
    return [part.astype(BF16) for part in parts]


def each(count, body):
    if count <= 4:
        for index in range(count):
            body(index)
    else:

        def step(index, _):
            body(index)
            return 0

        lax.fori_loop(0, count, step, 0)


def kernel(
    seq_count,
    hops,
    patches,
    grid,
    vqkv,
    vout,
    merge,
    block,
    offset,
    tokens,
    lengths,
    tqkv,
    tout,
    out,
    patch_v,
    vqkv_v,
    vout_v,
    merge_v,
    tqkv_v,
    tout_v,
    tok_v,
    meta_v,
    context_v,
    context_got,
    cross_send,
    cross_got,
    term_v,
    term_send,
    term_got,
    gathered,
    chosen_v,
    cells_normed,
    patch_query,
    normed_v,
    prompt_v,
    query_v,
    key_v,
    value_v,
    text_context,
    text_got,
    last_send,
    last_got,
    load_sem,
    weight_s,
    weight_r,
    tok_across_s,
    tok_across_r,
    tok_seq_s,
    tok_seq_r,
    tok_side_s,
    tok_side_r,
    meta_s,
    meta_r,
    half_s,
    half_r,
    cross_s,
    cross_r,
    term_s,
    term_r,
    gather_s,
    gather_r,
    relay_s,
    relay_r,
    chosen_s,
    chosen_r,
    last_s,
    last_r,
):
    me = lax.axis_index("seq")
    t = lax.axis_index("tp")
    tp = 4
    rows = tokens.shape[1]
    blocks = hops + 1
    sibling = t + 1 - 2 * lax.rem(t, 2)
    across = lax.rem(t + 2, 4)
    opposite = 3 - t
    partner = me + 1 - 2 * lax.rem(me, 2)

    def load(source, target, index):
        copy = pltpu.make_async_copy(source, target, load_sem.at[index])
        copy.start()
        return copy

    def remote(source, target, send, recv, device):
        return pltpu.make_async_remote_copy(
            src_ref=source,
            dst_ref=target,
            send_sem=send,
            recv_sem=recv,
            device_id=device,
            device_id_type=pl.DeviceIdType.MESH,
        )

    def to_tp(source, target, send, recv, peer):
        return remote(source, target, send, recv, (me, peer))

    def to_seq(source, target, send, recv, peer):
        return remote(source, target, send, recv, (peer, t))

    load_patches = load(patches.at[0], patch_v, 0)
    load_vqkv = load(vqkv, vqkv_v, 1)

    barrier = pltpu.get_barrier_semaphore()
    for d in range(1, tp):
        pl.semaphore_signal(
            barrier, inc=1, device_id=(me, lax.rem(t + d, tp)), device_id_type=pl.DeviceIdType.MESH
        )

    def greet(d, _):
        pl.semaphore_signal(
            barrier,
            inc=1,
            device_id=(lax.rem(me + d, seq_count), t),
            device_id_type=pl.DeviceIdType.MESH,
        )
        return 0

    lax.fori_loop(1, seq_count, greet, 0)

    half_rows, half_cols = grid[0, 0], grid[0, 1]
    count = patch_v.shape[0]
    slot = lax.broadcasted_iota(jnp.int32, (count, count), 0)
    cell = slot % MERGED
    part = slot // MERGED
    source = (2 * (cell // 8) + part // 2) * MAXGRID + 2 * (cell % 8) + part % 2
    order = (source == lax.broadcasted_iota(jnp.int32, (count, count), 1)).astype(F32).astype(BF16)
    load_patches.wait()
    picture = matmul(order, patch_v[...]).astype(BF16)
    patch_v[...] = picture
    normed = normalize(picture)
    key_slot = lax.broadcasted_iota(jnp.int32, (1, count), 1)
    key_cell = key_slot % MERGED
    key_allowed = (key_cell // 8 < half_rows) & (key_cell % 8 < half_cols)
    load_vqkv.wait()
    load_tokens = load(tokens, tok_v.at[0, t], 6)
    load_vout = load(vout, vout_v.at[0], 2)
    load_merge = load(merge.at[0], merge_v, 3)
    load_tqkv = load(tqkv, tqkv_v, 4)
    load_tout = load(tout, tout_v.at[0], 5)
    patch_query[...] = matmul_rows(normed, vqkv_v[0]).astype(BF16)
    keys = matmul_rows(normed, vqkv_v[1]).astype(BF16)
    values = matmul_rows(normed, vqkv_v[2]).astype(BF16)

    field = lax.broadcasted_iota(jnp.int32, (8, 128), 0)
    meta_v[me] = jnp.where(
        field == 0,
        half_rows,
        jnp.where(field == 1, half_cols, jnp.where(field == 2, block[0], offset[0])),
    )
    pl.semaphore_wait(barrier, tp - 1 + seq_count - 1)
    vout_copy = to_tp(vout, vout_v.at[1], weight_s.at[0], weight_r.at[0], sibling)
    vout_copy.start()
    tok_across = to_tp(tokens, tok_v.at[0, t], tok_across_s.at[0], tok_across_r.at[0], across)
    tok_across.start()

    def meta_copy(d):
        return to_seq(
            meta_v.at[me], meta_v.at[me], meta_s.at[d], meta_r.at[d], lax.rem(me + d, seq_count)
        )

    def send_meta(d, _):
        meta_copy(d).start()
        return 0

    lax.fori_loop(1, seq_count, send_meta, 0)

    def patch_rows(which):
        return pl.ds(pl.multiple_of(which * MERGED, MERGED), MERGED)

    def attend_patches(first, second):
        pair = (first, second)
        asking = jnp.concatenate([patch_query[patch_rows(which), :] for which in pair], axis=0)
        for index, piece in enumerate(attention(asking, keys, values, key_allowed)):
            lanes = pl.ds(index * 128, piece.shape[1])
            for place, which in enumerate(pair):
                context_v[patch_rows(which), lanes] = piece[place * MERGED : (place + 1) * MERGED]

    def share_context(index, which):
        copy = to_tp(
            context_v.at[patch_rows(which), :],
            context_got.at[index],
            half_s.at[index],
            half_r.at[index],
            sibling,
        )
        copy.start()
        return copy

    attend_patches(opposite, across)
    half_copies = [share_context(1, opposite)]
    load_vout.wait()
    far = matmul(context_v[patch_rows(across), :], vout_v[0])
    vout_copy.wait_recv()
    half_copies[0].wait_recv()
    cross_send[...] = (far + matmul(context_got[1], vout_v[1])).astype(BF16)
    cross = to_tp(cross_send, cross_got, cross_s.at[0], cross_r.at[0], across)
    cross.start()
    tout_copy = to_tp(tout, tout_v.at[1], weight_s.at[1], weight_r.at[1], sibling)
    tout_copy.start()
    load_tokens.wait()
    tok_across.wait_recv()

    def tok_seq_copy(hop, index):
        piece = t if index == 0 else across
        return to_seq(
            tok_v.at[0, piece],
            tok_v.at[hop, piece],
            tok_seq_s.at[hop, index],
            tok_seq_r.at[hop, index],
            lax.rem(me + hop, seq_count),
        )

    def tok_side_copy(hop, index):
        piece = t if index == 0 else across
        return to_tp(
            tok_v.at[hop, piece],
            tok_v.at[hop, piece],
            tok_side_s.at[hop, index],
            tok_side_r.at[hop, index],
            sibling,
        )

    def send_tokens(hop):
        for index in range(2):
            tok_seq_copy(hop + 1, index).start()

    each(hops, send_tokens)
    for index in range(2):
        tok_side_copy(0, index).start()

    attend_patches(sibling, t)
    half_copies.append(share_context(0, sibling))
    near = matmul(context_v[patch_rows(t), :], vout_v[0])
    half_copies[1].wait_recv()
    near = near + matmul(context_got[0], vout_v[1])
    hidden = patch_v[patch_rows(t), :].astype(F32) + near

    load_merge.wait()
    cross.wait_recv()
    merged_in = normalize(hidden + cross_got[...].astype(F32))

    share = MERGED // tp
    term_v[...] = matmul(merged_in, merge_v[...])
    term_copies = []
    for d in (2, 3, 1):
        peer = lax.rem(t + d, tp)
        term_send[d] = term_v[pl.ds(pl.multiple_of(peer * share, share), share), :].astype(BF16)
        copy = to_tp(term_send.at[d], term_got.at[d], term_s.at[d], term_r.at[d], peer)
        copy.start()
        term_copies.append(copy)

    def side_tokens(hop):
        for index in range(2):
            tok_seq_copy(hop + 1, index).wait()
            tok_side_copy(hop + 1, index).start()

    def tokens_in(hop):
        for index in range(2):
            tok_side_copy(hop, index).wait()

    same = (
        lax.broadcasted_iota(jnp.int32, (rows, rows), 0)
        == lax.broadcasted_iota(jnp.int32, (rows, rows), 1)
    )
    same = same.astype(F32).astype(BF16)

    def block_rows(hop):
        return pl.ds(pl.multiple_of(hop * rows, rows), rows)

    def norm_tokens(hop):
        whole_rows = matmul_rows(same, tok_v[hop].reshape(-1, rows))
        normed_v[block_rows(hop), :] = normalize(whole_rows)
        return whole_rows

    tokens_in(0)
    prompt_v[...] = norm_tokens(0).astype(BF16)
    merged = term_v[pl.ds(pl.multiple_of(t * share, share), share), :]
    for copy, d in zip(term_copies, (2, 3, 1)):
        copy.wait_recv()
        merged = merged + term_got[d].astype(F32)
    gathered[me] = merged.astype(BF16)

    def gather_copy(d):
        return to_seq(
            gathered.at[me],
            gathered.at[me],
            gather_s.at[d],
            gather_r.at[d],
            lax.rem(me + 2 * d, seq_count),
        )

    def relay_copy(d):
        piece = lax.rem(me + seq_count - 2 * d, seq_count)
        return to_seq(
            gathered.at[piece], gathered.at[piece], relay_s.at[d], relay_r.at[d], partner
        )

    def send_merged(d):
        gather_copy(d + 1).start()

    each(seq_count // 2 - 1, send_merged)
    relay_copy(0).start()

    each(hops, side_tokens)
    load_tqkv.wait()
    query_v[...] = matmul_rows(normed_v[0:rows, :], tqkv_v[0]).astype(BF16)

    def relay(d):
        gather_copy(d + 1).wait_recv()
        relay_copy(d + 1).start()

    def norm_earlier(hop):
        tokens_in(hop + 1)
        norm_tokens(hop + 1)

    each(seq_count // 2 - 1, relay)
    each(hops, norm_earlier)
    group = 3 if blocks % 3 == 0 else 1

    def project(index):
        some = pl.ds(pl.multiple_of(index * group * rows, rows), group * rows)
        key_v[some, :] = matmul_rows(normed_v[some, :], tqkv_v[1]).astype(BF16)
        value_v[some, :] = matmul_rows(normed_v[some, :], tqkv_v[2]).astype(BF16)

    each(blocks // group, project)
    half = rows // 2
    core = lax.rem(t, 2)

    def visible_keys():
        position = lax.broadcasted_iota(jnp.int32, (rows, 1), 0) + me * rows
        start = jnp.zeros((rows, 1), jnp.int32)
        end = jnp.int32(0)
        for index in range(lengths.shape[0]):
            end = end + lengths[index]
            start = jnp.where(end <= position, end, start)
        lane = lax.broadcasted_iota(jnp.int32, (1, blocks * rows), 1)
        key_position = (me - lane // rows) * rows + lane % rows
        return (key_position <= position) & (key_position >= start)

    def meta_arrived(d, _):
        meta_copy(d).wait()
        return 0

    lax.fori_loop(1, seq_count, meta_arrived, 0)

    def relayed(d):
        relay_copy(d).wait_recv()

    each(seq_count // 2, relayed)

    def choose(hop):
        def add(index, cells_sum):
            hit = (meta_v[index][2:3, 0:1] == me - hop).astype(F32)
            return cells_sum + gathered[index].astype(F32) * hit

        cells_sum = jnp.zeros((share, patch_v.shape[1]), F32)
        if seq_count <= 8:
            for index in range(seq_count):
                cells_sum = add(index, cells_sum)
        else:
            cells_sum = lax.fori_loop(0, seq_count, add, cells_sum)
        chosen_v[t, pl.ds(pl.multiple_of(hop * share, share), share), :] = cells_sum.astype(BF16)

    each(blocks, choose)

    def chosen_copy(index, piece, peer):
        return to_tp(
            chosen_v.at[piece], chosen_v.at[piece], chosen_s.at[index], chosen_r.at[index], peer
        )

    chosen_copies = [chosen_copy(0, t, across), chosen_copy(1, t, sibling)]
    for copy in chosen_copies:
        copy.start()

    all_cells = blocks * MERGED
    lane = lax.broadcasted_iota(jnp.int32, (1, all_cells), 1)
    lane_hop = lane % (blocks * share) // share
    lane_cell = lane // (blocks * share) * share + lane % share
    row_cell, col_cell = lane_cell // 8, lane_cell % 8

    def placement(hop):
        def add(index, state):
            about, present = state
            hit = (meta_v[index][2:3, :] == me - hop).astype(jnp.int32)
            return about + meta_v[index] * hit, present + hit

        about, present = lax.fori_loop(
            0, seq_count, add, (jnp.zeros((8, 128), jnp.int32), jnp.zeros((1, 128), jnp.int32))
        )
        g0, g1 = about[0:1, 0:1], about[1:2, 0:1]
        usable = (row_cell < g0) & (col_cell < g1) & (present[:, 0:1] > 0) & (lane_hop == hop)
        target = jnp.where(usable, about[3:4, 0:1] + row_cell * g1 + col_cell, -1)
        table = (lax.broadcasted_iota(jnp.int32, (rows, all_cells), 0) == target).astype(F32)
        return table.astype(BF16), jnp.max(table, axis=1, keepdims=True)

    if blocks <= 4:
        placements = [placement(hop) for hop in range(blocks)]

    def placement_of(hop):
        return placements[hop] if blocks <= 4 else placement(hop)

    cells_normed[t] = normalize(chosen_v[t])
    chosen_copies[1].wait_recv()
    cells_normed[sibling] = normalize(chosen_v[sibling])
    chosen_copies[0].wait_recv()
    chosen_copies.append(chosen_copy(2, across, sibling))
    chosen_copies[2].start()
    cells_normed[across] = normalize(chosen_v[across])
    chosen_copies[2].wait_recv()
    cells_normed[opposite] = normalize(chosen_v[opposite])
    normed = cells_normed[...].reshape(all_cells, -1)
    query_cells = matmul_rows(normed, tqkv_v[0]).astype(BF16)
    key_cells = matmul_rows(normed, tqkv_v[1]).astype(BF16)
    value_cells = matmul_rows(normed, tqkv_v[2]).astype(BF16)

    def put(table, covered, cells_here, before):
        return jnp.where(
            covered > 0, matmul(table, cells_here), before.astype(F32)
        ).astype(BF16)

    def put_block(hop):
        table, covered = placement_of(hop)
        here = block_rows(hop)
        key_v[here, :] = put(table, covered, key_cells, key_v[here, :])
        value_v[here, :] = put(table, covered, value_cells, value_v[here, :])

    each(blocks, put_block)
    table, covered = placement_of(0)
    query_v[...] = put(table, covered, query_cells, query_v[...])

    own_half = pl.ds(pl.multiple_of(core * half, half), half)
    side_half = pl.ds(pl.multiple_of((1 - core) * half, half), half)

    def attend_rows(here):
        visible = visible_keys()
        pieces = attention(query_v[here, :], key_v[...], value_v[...], visible)
        for index, piece in enumerate(pieces):
            text_context[here, pl.ds(index * 128, piece.shape[1])] = piece

    attend_rows(pl.ds(0, rows))
    side = to_tp(text_context.at[side_half, :], text_got, last_s.at[0], last_r.at[0], sibling)
    side.start()
    load_tout.wait()
    summed = matmul(text_context[own_half, :], tout_v[0])
    tout_copy.wait_recv()
    side.wait_recv()
    summed = (summed + matmul(text_got[...], tout_v[1])).astype(BF16)
    last_send[...] = summed
    last = to_tp(last_send, last_got, last_s.at[1], last_r.at[1], across)
    last.start()
    prompt_v[...] = put(table, covered, chosen_v[...].reshape(all_cells, -1), prompt_v[...])
    residual = prompt_v[own_half, :].astype(F32)
    last.wait_recv()
    total = summed.astype(F32) + last_got[...].astype(F32)
    out[own_half, :] = (residual + total).astype(BF16)
    done = to_tp(
        out.at[own_half, :], out.at[own_half, :], last_s.at[2], last_r.at[2], sibling
    )
    done.start()

    def sent(d):
        gather_copy(d + 1).wait_send()

    each(seq_count // 2 - 1, sent)

    def handed_on(d):
        relay_copy(d).wait_send()

    each(seq_count // 2, handed_on)
    for copy in [vout_copy, tout_copy, tok_across, cross, side, last]:
        copy.wait_send()
    for copy in half_copies + term_copies + chosen_copies:
        copy.wait_send()
    done.wait()


def local(
    seq_count,
    patches,
    picture_grid,
    vision_qkv,
    vision_out,
    merge_weight,
    picture_block,
    picture_offset,
    tokens,
    prompt_lengths,
    text_qkv,
    text_out,
):
    hops = (seq_count + 3) // 4
    blocks = hops + 1
    count, model = patches.shape[1:]
    rows, width = tokens.shape
    share, half = MERGED // 4, rows // 2
    dma = pltpu.SemaphoreType.DMA
    hbm = pl.BlockSpec(memory_space=pltpu.HBM)
    scalars = pl.BlockSpec(memory_space=pltpu.SMEM)
    vmem = pl.BlockSpec(memory_space=pltpu.VMEM)
    return pl.pallas_call(
        functools.partial(kernel, seq_count, hops),
        out_shape=pltpu.VMEM((rows, model), BF16),
        in_specs=[hbm, scalars, hbm, hbm, hbm, scalars, scalars, hbm, scalars, hbm, hbm],
        out_specs=vmem,
        scratch_shapes=[
            pltpu.VMEM((count, model), BF16),
            pltpu.VMEM((3, width, model), BF16),
            pltpu.VMEM((2, width, model), BF16),
            pltpu.VMEM((model, model), BF16),
            pltpu.VMEM((3, width, model), BF16),
            pltpu.VMEM((2, width, model), BF16),
            pltpu.VMEM((blocks, 4, width, rows), BF16),
            pltpu.VMEM((seq_count, 8, 128), jnp.int32),
            pltpu.VMEM((count, width), BF16),
            pltpu.VMEM((2, MERGED, width), BF16),
            pltpu.VMEM((MERGED, model), BF16),
            pltpu.VMEM((MERGED, model), BF16),
            pltpu.VMEM((MERGED, model), F32),
            pltpu.VMEM((4, share, model), BF16),
            pltpu.VMEM((4, share, model), BF16),
            pltpu.VMEM((seq_count, share, model), BF16),
            pltpu.VMEM((4, blocks * share, model), BF16),
            pltpu.VMEM((4, blocks * share, model), BF16),
            pltpu.VMEM((count, width), BF16),
            pltpu.VMEM((blocks * rows, model), BF16),
            pltpu.VMEM((rows, model), BF16),
            pltpu.VMEM((rows, width), BF16),
            pltpu.VMEM((blocks * rows, width), BF16),
            pltpu.VMEM((blocks * rows, width), BF16),
            pltpu.VMEM((rows, width), BF16),
            pltpu.VMEM((half, width), BF16),
            pltpu.VMEM((half, model), BF16),
            pltpu.VMEM((half, model), BF16),
            dma((7,)),
            dma((2,)),
            dma((2,)),
            dma((1,)),
            dma((1,)),
            dma((blocks, 2)),
            dma((blocks, 2)),
            dma((blocks, 2)),
            dma((blocks, 2)),
            dma((seq_count,)),
            dma((seq_count,)),
            dma((2,)),
            dma((2,)),
            dma((1,)),
            dma((1,)),
            dma((4,)),
            dma((4,)),
            dma((seq_count,)),
            dma((seq_count,)),
            dma((seq_count,)),
            dma((seq_count,)),
            dma((3,)),
            dma((3,)),
            dma((3,)),
            dma((3,)),
        ],
        compiler_params=pltpu.CompilerParams(
            collective_id=0, has_side_effects=True, vmem_limit_bytes=56 * 1024 * 1024
        ),
    )(
        patches,
        picture_grid,
        jnp.transpose(vision_qkv, (1, 2, 0)),
        vision_out,
        merge_weight,
        picture_block,
        picture_offset,
        tokens.T,
        prompt_lengths,
        jnp.transpose(text_qkv, (1, 2, 0)),
        text_out,
    )


def solution(mesh):
    placed = (
        P("seq", None, None),
        P("seq", None),
        P(None, None, "tp"),
        P("tp", None),
        P("tp", None, None),
        P("seq"),
        P("seq"),
        P("seq", "tp"),
        P(),
        P(None, None, "tp"),
        P("tp", None),
    )
    return jax.shard_map(
        functools.partial(local, mesh.shape["seq"]),
        mesh=mesh,
        in_specs=placed,
        out_specs=P("seq", None),
        check_vma=False,
    )
```
